32 devices in a mesh: dp: 8 (over z, y), mp: 4 (over x, core).
Axes of the slice: x: 2, y: 2, z: 4, core: 2. Of those that a mesh axis runs over, the one named last changes fastest.
Arguments:
- latents: float32 [16, 20, 1024], P('dp', None, 'mp'), may hold values from -6 to 6
- noise_draw: float32 [16, 20, 1024], P('dp', None, 'mp'), may hold values from -6 to 6
- timesteps: int32 [16], P('dp'), may hold values from 60 to 519
- text_ids: int32 [16, 128], P('dp'), may hold values from 0 to 32127
- text_len: int32 [16], P('dp'), may hold values from 1 to 128, as said below
- item_counts: int32 [8], P('dp'), may hold values from 1 to 2, as said below
- text_table: bfloat16 [32128, 768], P('mp'), may hold values from -6 to 6
- io_weight: float32 [2, 20, 1024], P(None, None, 'dp'), may hold values from -4 to 4
- io_first: float32 [2, 20, 1024], P(None, None, 'dp'), may hold values from -2.9802322e-07 to 2.9802322e-07
- io_second: float32 [2, 20, 1024], P(None, None, 'dp'), may hold values from 3.0718206e-17 to 1.2287282e-16
- io_average: float32 [2, 20, 1024], P(None, None, 'dp'), may hold values from -4 to 4
- norm_gains: float32 [7, 1024], P(None, 'dp'), may hold values from 0.2 to 3
- gains_first: float32 [7, 1024], P(None, 'dp'), may hold values from -1.1920929e-06 to 1.1920929e-06
- gains_second: float32 [7, 1024], P(None, 'dp'), may hold values from 4.914913e-16 to 1.9659652e-15
- gains_average: float32 [7, 1024], P(None, 'dp'), may hold values from 0.2 to 3
- col_weight: float32 [2, 1024, 8, 1024], P(None, 'dp', None, 'mp'), may hold values from -0.1875 to 0.1875
- col_first: float32 [2, 1024, 8, 1024], P(None, 'dp', None, 'mp'), may hold values from -2.9802322e-07 to 2.9802322e-07
- col_second: float32 [2, 1024, 8, 1024], P(None, 'dp', None, 'mp'), may hold values from 3.0718206e-17 to 1.2287282e-16
- col_average: float32 [2, 1024, 8, 1024], P(None, 'dp', None, 'mp'), may hold values from -0.1875 to 0.1875
- text_weight: float32 [2, 768, 2, 1024], P(None, 'dp', None, 'mp'), may hold values from -0.21875 to 0.21875
- text_first: float32 [2, 768, 2, 1024], P(None, 'dp', None, 'mp'), may hold values from -2.9802322e-07 to 2.9802322e-07
- text_second: float32 [2, 768, 2, 1024], P(None, 'dp', None, 'mp'), may hold values from 3.0718206e-17 to 1.2287282e-16
- text_average: float32 [2, 768, 2, 1024], P(None, 'dp', None, 'mp'), may hold values from -0.21875 to 0.21875
- row_weight: float32 [2, 6, 1024, 1024], P(None, None, 'dp', 'mp'), may hold values from -3 to 3
- row_first: float32 [2, 6, 1024, 1024], P(None, None, 'dp', 'mp'), may hold values from -2.9802322e-07 to 2.9802322e-07
- row_second: float32 [2, 6, 1024, 1024], P(None, None, 'dp', 'mp'), may hold values from 3.8397757e-18 to 1.5359103e-17
- row_average: float32 [2, 6, 1024, 1024], P(None, None, 'dp', 'mp'), may hold values from -3 to 3
Outputs:
- loss_sum: float32 [], replicated
- item_total: float32 [], replicated
- grad_norm: float32 [], replicated
- io_weight_new: float32 [2, 20, 1024], P(None, None, 'dp')
- io_first_new: float32 [2, 20, 1024], P(None, None, 'dp')
- in_second_new: float32 [20, 1024], P(None, 'dp')
- out_second_new: float32 [20, 1024], P(None, 'dp')
- io_average_new: float32 [2, 20, 1024], P(None, None, 'dp')
- norm_gains_new: float32 [7, 1024], P(None, 'dp')
- gains_first_new: float32 [7, 1024], P(None, 'dp')
- gains_second_new: float32 [7, 1024], P(None, 'dp')
- gains_average_new: float32 [7, 1024], P(None, 'dp')
- col_weight_new: float32 [2, 1024, 8, 1024], P(None, 'dp', None, 'mp')
- col_first_new: float32 [2, 1024, 8, 1024], P(None, 'dp', None, 'mp')
- col_second_new: float32 [2, 1024, 8, 1024], P(None, 'dp', None, 'mp')
- col_average_new: float32 [2, 1024, 8, 1024], P(None, 'dp', None, 'mp')
- text_weight_new: float32 [2, 768, 2, 1024], P(None, 'dp', None, 'mp')
- text_first_new: float32 [2, 768, 2, 1024], P(None, 'dp', None, 'mp')
- text_second_new: float32 [2, 768, 2, 1024], P(None, 'dp', None, 'mp')
- text_average_new: float32 [2, 768, 2, 1024], P(None, 'dp', None, 'mp')
- row_weight_new: float32 [2, 6, 1024, 1024], P(None, None, 'dp', 'mp')
- row_first_new: float32 [2, 6, 1024, 1024], P(None, None, 'dp', 'mp')
- row_second_new: float32 [2, 6, 1024, 1024], P(None, None, 'dp', 'mp')
- row_average_new: float32 [2, 6, 1024, 1024], P(None, None, 'dp', 'mp')
The draws below stay inside these ranges and needn't reach their ends.
Inputs may be any that keep to these rules, and one draw needn't show every extreme that they name: `text_len`: some item of the batch has all 128 caption tokens. `item_counts`: some index of dp holds 2 real items; real items take the lowest slots.
All inputs are finite; a program needn't handle non-finite values.
Results may differ from the reference program's by a relative error of at most 0.018.
Values may be sent and summed in bfloat16 or wider, within the bound.
A program may use at most 384 MiB of HBM per device.

```python
import math
import jax
import jax.numpy as jnp
import numpy as np
from jax import lax

HEADS = 16
HEAD_DIM = 64
D = 1024
CH = 20
TD = 768
VOCAB = 32128
TXT = 128
FRAMES = 1024
ITEMS_DEV = 2
LAYERS = 2
STEP = 10
ITEMS = 16
GN = 7
NPARAM = 32553984


def clipped_normal(key, shape):
    return jnp.clip(jax.random.normal(key, shape, jnp.float32), -3.0, 3.0)


def io_scaled(base_draw):
    scales = jnp.array([CH ** (-0.5), D ** (-0.5)], jnp.float32)
    return base_draw * scales[:, None, None]


def row_scaled(base_draw):
    down_scale = (4.0 * D) ** (-0.5)
    scales = jnp.array([(FRAMES / (3.0 * D)) ** 0.5, (TXT / (3.0 * D)) ** 0.5, down_scale, down_scale, down_scale, down_scale], jnp.float32)
    return base_draw * scales[None, :, None, None]


def gain_scaled(base_draw, lowest, highest):
    ramp_line = lowest + (highest - lowest) * jnp.arange(D, dtype=jnp.float32) / (D - 1)
    return ramp_line[None, :] * (1.0 + 0.15 * base_draw)


def draw_timesteps(key, part):
    key = jax.random.fold_in(key, 11)
    groups = ITEMS // ITEMS_DEV
    owner_index = jnp.arange(ITEMS, dtype=jnp.int32) // ITEMS_DEV
    offset = 60 + 400 * owner_index // max(groups - 1, 1)
    values = offset + jax.random.randint(key, (ITEMS,), 0, 60, jnp.int32)
    return values.at[0].set(60).at[ITEMS - 1].set(519)


def draw_text_len(key, part):
    key = jax.random.fold_in(key, 12)
    first_key, second_key = jax.random.split(key)
    lengths = jax.random.randint(first_key, (ITEMS,), 1, TXT + 1, jnp.int32)
    chosen = jax.random.randint(second_key, (), 0, ITEMS, jnp.int32)
    return lengths.at[chosen].set(TXT)


def draw_item_counts(key, part):
    key = jax.random.fold_in(key, 13)
    groups = ITEMS // ITEMS_DEV
    first_key, second_key = jax.random.split(key)
    counts = jax.random.randint(first_key, (groups,), 1, ITEMS_DEV + 1, jnp.int32)
    chosen = jax.random.randint(second_key, (), 0, groups, jnp.int32)
    return counts.at[chosen].set(ITEMS_DEV)


def draw_io_weight(key, part):
    key = jax.random.fold_in(key, 21)
    base_draw = clipped_normal(key, (2, CH, D))
    return io_scaled(base_draw)


def draw_io_average(key, part):
    key = jax.random.fold_in(key, 22)
    base_draw = clipped_normal(key, (2, CH, D))
    return io_scaled(base_draw)


def draw_norm_gains(key, part):
    key = jax.random.fold_in(key, 31)
    return gain_scaled(clipped_normal(key, (GN, D)), 0.6, 1.8)


def draw_gains_average(key, part):
    key = jax.random.fold_in(key, 32)
    return gain_scaled(clipped_normal(key, (GN, D)), 0.6, 1.8)


def draw_row_weight(key, part):
    key = jax.random.fold_in(key, 41)
    base_draw = clipped_normal(key, (LAYERS, 6, D, D))
    return row_scaled(base_draw)


def draw_row_average(key, part):
    key = jax.random.fold_in(key, 42)
    base_draw = clipped_normal(key, (LAYERS, 6, D, D))
    return row_scaled(base_draw)


def plant(drawn, rng, low, top_value):
    longest = drawn.shape.index(max(drawn.shape))
    spots = []
    for shift in (0, 1):
        where = [jax.random.randint(jax.random.fold_in(rng, axis), (), 0, length) for axis, length in enumerate(drawn.shape)]
        where[longest] = (where[longest] + shift) % drawn.shape[longest]
        spots.append(tuple(where))
    return drawn.at[spots[0]].set(low).at[spots[1]].set(top_value)


def block_levels(rng, extent, cuts, smallest, high):
    factor_of = 1.0
    for axis_at, shards_of in cuts:
        heights = jax.random.uniform(jax.random.fold_in(jax.random.fold_in(rng, 6), axis_at), (shards_of,), jnp.float32, smallest / len(cuts), high / len(cuts))
        factor_of = factor_of * jnp.repeat(jnp.exp(heights), extent[axis_at] // shards_of).reshape((-1,) + (1,) * (len(extent) - 1 - axis_at))
    return factor_of


def rank_bounds(count, lean):
    loads = [(1 << 20) // math.isqrt(rank ** lean) + 1 for rank in range(1, count + 1)]
    spread = 1 + sum(loads) // (1 << 30)
    return np.cumsum(np.array([max(1, weight // spread) for weight in loads]))


def skewed_ids(rng, dims, number_of, skew):
    table = rank_bounds(number_of, skew)
    pick = jax.random.randint(jax.random.fold_in(rng, 1), dims, 0, int(table[number_of - 1]))
    grade = jnp.searchsorted(jnp.asarray(table, jnp.int32), pick, side="right")
    return jax.random.permutation(jax.random.fold_in(rng, 2), number_of)[grade].astype(jnp.int32)


def centred(rng, shape, spread, limit, shards=(), held_as=jnp.bfloat16):
    factor_of = block_levels(rng, shape, shards, -0.22, 0.18) if shards else 1.0
    entries = jax.random.normal(rng, shape, jnp.float32) * spread * factor_of
    return jnp.minimum(jnp.maximum(entries, -limit), limit).astype(held_as)


def setup_inputs(seed: int = 0) -> dict:
    streams_of = jax.random.split(jax.random.key(seed), 28)
    return {
        "latents": centred(streams_of[0], (ITEMS, CH, FRAMES), 1.0, 6.0, ((0, 8), (2, 4)), jnp.float32),
        "noise_draw": centred(streams_of[1], (ITEMS, CH, FRAMES), 1.0, 6.0, ((0, 8), (2, 4)), jnp.float32),
        "timesteps": draw_timesteps(jax.random.fold_in(streams_of[27], 71), 0),
        "text_ids": plant(skewed_ids(streams_of[3], (ITEMS, TXT), VOCAB, 2), jax.random.fold_in(streams_of[3], 3), 0, VOCAB - 1).astype(jnp.int32),
        "text_len": draw_text_len(jax.random.fold_in(streams_of[27], 71), 0),
        "item_counts": draw_item_counts(jax.random.fold_in(streams_of[27], 71), 0),
        "text_table": centred(streams_of[6], (VOCAB, TD), 1.0, 6.0, ((0, 4),)),
        "io_weight": draw_io_weight(jax.random.fold_in(streams_of[27], 71), 0),
        "io_first": centred(streams_of[8], (2, CH, D), (0.000111 * NPARAM ** -0.5), 2.980232238769531e-07, ((2, 8),), jnp.float32),
        "io_second": jnp.clip(jnp.exp(math.log(1.2287282279019535e-16) - 1.3862944 * jax.random.uniform(streams_of[9], (2, CH, D), jnp.float32) ** block_levels(streams_of[9], (2, CH, D), ((2, 8),), -0.2, 0.2)), 3.071820569754884e-17, 1.2287282279019535e-16),
        "io_average": draw_io_average(jax.random.fold_in(streams_of[27], 71), 0),
        "norm_gains": draw_norm_gains(jax.random.fold_in(streams_of[27], 71), 0),
        "gains_first": centred(streams_of[12], (GN, D), (0.000444 * NPARAM ** -0.5), 1.1920928955078125e-06, ((1, 8),), jnp.float32),
        "gains_second": jnp.clip(jnp.exp(math.log(1.9659651646431256e-15) - 1.3862944 * jax.random.uniform(streams_of[13], (GN, D), jnp.float32) ** block_levels(streams_of[13], (GN, D), ((1, 8),), -0.2, 0.2)), 4.914912911607814e-16, 1.9659651646431256e-15),
        "gains_average": draw_gains_average(jax.random.fold_in(streams_of[27], 71), 0),
        "col_weight": centred(streams_of[15], (LAYERS, D, 8, D), D ** -0.5, 0.1875, ((1, 8), (3, 4)), jnp.float32),
        "col_first": centred(streams_of[16], (LAYERS, D, 8, D), (0.000111 * NPARAM ** -0.5), 2.980232238769531e-07, ((1, 8), (3, 4)), jnp.float32),
        "col_second": jnp.clip(jnp.exp(math.log(1.2287282279019535e-16) - 1.3862944 * jax.random.uniform(streams_of[17], (LAYERS, D, 8, D), jnp.float32) ** block_levels(streams_of[17], (LAYERS, D, 8, D), ((1, 8), (3, 4)), -0.2, 0.2)), 3.071820569754884e-17, 1.2287282279019535e-16),
        "col_average": centred(streams_of[18], (LAYERS, D, 8, D), D ** -0.5, 0.1875, ((1, 8), (3, 4)), jnp.float32),
        "text_weight": centred(streams_of[19], (LAYERS, TD, 2, D), TD ** -0.5, 0.21875, ((1, 8), (3, 4)), jnp.float32),
        "text_first": centred(streams_of[20], (LAYERS, TD, 2, D), (0.000111 * NPARAM ** -0.5), 2.980232238769531e-07, ((1, 8), (3, 4)), jnp.float32),
        "text_second": jnp.clip(jnp.exp(math.log(1.2287282279019535e-16) - 1.3862944 * jax.random.uniform(streams_of[21], (LAYERS, TD, 2, D), jnp.float32) ** block_levels(streams_of[21], (LAYERS, TD, 2, D), ((1, 8), (3, 4)), -0.2, 0.2)), 3.071820569754884e-17, 1.2287282279019535e-16),
        "text_average": centred(streams_of[22], (LAYERS, TD, 2, D), TD ** -0.5, 0.21875, ((1, 8), (3, 4)), jnp.float32),
        "row_weight": draw_row_weight(jax.random.fold_in(streams_of[27], 71), 0),
        "row_first": centred(streams_of[24], (LAYERS, 6, D, D), (0.000111 * NPARAM ** -0.5), 2.980232238769531e-07, ((2, 8), (3, 4)), jnp.float32),
        "row_second": jnp.clip(jnp.exp(math.log(1.535910284877442e-17) - 1.3862944 * jax.random.uniform(streams_of[25], (LAYERS, 6, D, D), jnp.float32) ** block_levels(streams_of[25], (LAYERS, 6, D, D), ((2, 8), (3, 4)), -0.2, 0.2)), 3.839775712193605e-18, 1.535910284877442e-17),
        "row_average": draw_row_average(jax.random.fold_in(streams_of[27], 71), 0),
    }


@jax.custom_vjp
def low(v):
    return lax.optimization_barrier(v.astype(jnp.bfloat16)).astype(jnp.float32)

@jax.custom_vjp
def low_back(v):
    return v

def low_keep(v):
    return (low(v), None)

def low_pass(kept, grad):
    return (grad,)

def back_keep(v):
    return (v, None)

def back_low(kept, grad):
    return (low(grad),)
low.defvjp(low_keep, low_pass)
low_back.defvjp(back_keep, back_low)
highest = lax.Precision.HIGHEST
norm_eps = 1e-06
clip_limit = 0.001
matrix_rate = 0.04
gain_rate = 0.6
row_rate = 0.1
beta_first = 0.9
beta_second = 0.999
adam_eps = 1e-08
weight_decay = 0.01
average_keep = 0.5
snr_limit = 5.0

def round_both(tensor):
    return low(low_back(tensor))

def sinusoid(position, width):
    half_width = width // 2
    frequency = jnp.exp(-math.log(10000.0) * jnp.arange(half_width, dtype=jnp.float32) / half_width)
    angles = position[..., None] * frequency
    return jnp.concatenate([jnp.sin(angles), jnp.cos(angles)], axis=-1)

def plan():
    beta_table = jnp.linspace(0.00085 ** 0.5, 0.012 ** 0.5, 1000, dtype=jnp.float32) ** 2
    return jnp.cumprod(1.0 - beta_table)

def layer_norm(inputs, gain):
    centre = inputs - lax.optimization_barrier(jnp.mean(inputs, -1, keepdims=True))
    inverse = lax.rsqrt(lax.optimization_barrier(jnp.mean(centre * centre, -1, keepdims=True)) + norm_eps)
    return centre * inverse * gain

def attend(queries, keys_in, values_in, allowed):
    scores = low_back(jnp.einsum('qhe,khe->hqk', queries, keys_in, precision=highest) * HEAD_DIM ** (-0.5))
    scores = jnp.where(allowed[None, None, :], scores, -1e+30)
    probs_full = jax.nn.softmax(scores, axis=-1)
    return round_both(jnp.einsum('hqk,khe->qhe', low(probs_full), values_in, precision=highest))

def item_loss(weights, alpha_table, latent, noise, step_index, text_feat, length, valid_item):
    io_w, gain_w, col_w, text_w, row_w = weights
    alpha = alpha_table[step_index]
    noisy = jnp.sqrt(alpha) * latent + jnp.sqrt(1.0 - alpha) * noise
    frame_pos = jnp.arange(FRAMES).astype(jnp.float32)
    resid = low_back(jnp.dot(low(noisy).T, io_w[0], precision=highest))
    resid = resid + sinusoid(frame_pos, D) + sinusoid(step_index.astype(jnp.float32), D)[None]
    allowed = jnp.arange(TXT) < length
    all_keys = jnp.ones((FRAMES,), bool)
    for layer_index in range(LAYERS):
        normed = low(layer_norm(resid, gain_w[3 * layer_index]))
        projected = round_both(jnp.einsum('fd,dsc->fsc', normed, col_w[layer_index, :, 0:3], precision=highest))
        split_heads = projected.reshape(FRAMES, 3, HEADS, HEAD_DIM)
        attended = attend(split_heads[:, 0], split_heads[:, 1], split_heads[:, 2], all_keys).reshape(FRAMES, D)
        resid = resid + low_back(jnp.einsum('fc,dc->fd', attended, row_w[layer_index, 0], precision=highest))
        normed = low(layer_norm(resid, gain_w[3 * layer_index + 1]))
        cross_query = round_both(jnp.dot(normed, col_w[layer_index, :, 3], precision=highest)).reshape(FRAMES, HEADS, HEAD_DIM)
        text_proj = round_both(jnp.einsum('td,dsc->tsc', text_feat, text_w[layer_index], precision=highest))
        text_heads = text_proj.reshape(TXT, 2, HEADS, HEAD_DIM)
        attended = attend(cross_query, text_heads[:, 0], text_heads[:, 1], allowed).reshape(FRAMES, D)
        resid = resid + low_back(jnp.einsum('fc,dc->fd', attended, row_w[layer_index, 1], precision=highest))
        normed = low(layer_norm(resid, gain_w[3 * layer_index + 2]))
        hidden = low_back(jnp.einsum('fd,dsc->fsc', normed, col_w[layer_index, :, 4:8], precision=highest))
        active = low(jax.nn.gelu(hidden, approximate=True))
        resid = resid + low_back(jnp.einsum('fsc,sdc->fd', active, row_w[layer_index, 2:6], precision=highest))
    final = low(layer_norm(resid, gain_w[3 * LAYERS]))
    predicted = low_back(jnp.dot(io_w[1], final.T, precision=highest))
    error = predicted - noise
    snr_ratio = alpha / (1.0 - alpha)
    return valid_item * (jnp.minimum(snr_ratio, snr_limit) / snr_ratio) * jnp.mean(error * error)

def adam_update(master, first_moment, second_moment, average, gradient, factor, step_rate):
    clipped = gradient * factor
    first_new = beta_first * first_moment + (1.0 - beta_first) * clipped
    second_new = beta_second * second_moment + (1.0 - beta_second) * clipped * clipped
    first_hat = first_new / (1.0 - beta_first ** STEP)
    second_hat = second_new / (1.0 - beta_second ** STEP)
    master_new = master - step_rate * (first_hat / (jnp.sqrt(second_hat) + adam_eps) + weight_decay * master)
    return (master_new, first_new, second_new, average_keep * average + (1.0 - average_keep) * master_new)

def reference(latents, noise_draw, timesteps, text_ids, text_len, item_counts, text_table, io_weight, io_first, io_second, io_average, norm_gains, gains_first, gains_second, gains_average, col_weight, col_first, col_second, col_average, text_weight, text_first, text_second, text_average, row_weight, row_first, row_second, row_average):
    alpha_table = plan()
    slot_index = jnp.arange(ITEMS)
    valid_items = (slot_index % ITEMS_DEV < item_counts[slot_index // ITEMS_DEV]).astype(jnp.float32)
    item_total = jnp.sum(item_counts).astype(jnp.float32)
    text_feat = text_table.astype(jnp.float32)[text_ids]
    masters = (io_weight, norm_gains, col_weight, text_weight, row_weight)

    def total_loss(params):
        weights = tuple((low(master) for master in params))

        def one_item(data):
            return item_loss(weights, alpha_table, *data)
        losses = lax.map(jax.checkpoint(one_item), (latents, noise_draw, timesteps, text_feat, text_len, valid_items))
        return jnp.sum(losses)
    loss_sum, pull_back = jax.vjp(total_loss, masters)
    grads = pull_back(jnp.ones((), jnp.float32) / item_total)[0]
    grad_norm = jnp.sqrt(sum((jnp.sum(entry * entry) for entry in grads)))
    factor = jnp.minimum(1.0, clip_limit / (grad_norm + 1e-06))
    firsts = (io_first, gains_first, col_first, text_first, row_first)
    seconds = (io_second, gains_second, col_second, text_second, row_second)
    averages = (io_average, gains_average, col_average, text_average, row_average)
    rates = (matrix_rate, gain_rate, matrix_rate, matrix_rate, row_rate)
    results = [loss_sum, item_total, grad_norm]
    for index in range(5):
        updated = adam_update(masters[index], firsts[index], seconds[index], averages[index], grads[index], factor, rates[index])
        if index == 0:
            results.extend([updated[0], updated[1], updated[2][0], updated[2][1], updated[3]])
        else:
            results.extend(updated)
    return tuple(results)
```

```python
import functools
import math

import jax
import jax.numpy as jnp
from jax import lax
from jax.experimental import pallas as pl
from jax.experimental.pallas import tpu as pltpu
from jax.sharding import PartitionSpec as P

HEAD_DIM = 64
STEP = 10
LANES = 128

norm_eps = 1e-06
clip_limit = 0.001
matrix_rate = 0.04
gain_rate = 0.6
row_rate = 0.1
beta_first = 0.9
beta_second = 0.999
adam_eps = 1e-08
weight_decay = 0.01
average_keep = 0.5
snr_limit = 5.0

score_scale = HEAD_DIM ** (-0.5)
log2_e = 1.4426950408889634
exp_scale = score_scale * log2_e
masked_score = -1e30


def as_low(tensor):
    return tensor.astype(jnp.bfloat16)


def plan():
    beta_table = jnp.linspace(0.00085**0.5, 0.012**0.5, 1000, dtype=jnp.float32) ** 2
    return jnp.cumprod(1.0 - beta_table)


def exchange(tensor, axis, mask):
    size = lax.axis_size(axis)
    return lax.ppermute(tensor, axis, [(i, i ^ mask) for i in range(size)])


class Layout:
    def __init__(self, items):
        self.dp_size = lax.axis_size("dp")
        self.mp_size = lax.axis_size("mp")
        self.ranks = self.mp_size // items
        self.item = lax.axis_index("mp") // self.ranks
        self.rank = lax.axis_index("mp") % self.ranks
        self.dp = lax.axis_index("dp")
        self.masks = []
        mask = self.dp_size >> 1
        while mask:
            self.masks.append(mask)
            mask >>= 1
        self.offsets = [
            sum(mask for bit, mask in enumerate(self.masks) if (place >> bit) & 1)
            for place in range(self.dp_size)
        ]

    def blocks(self):
        return jnp.bitwise_xor(self.dp, jnp.array(self.offsets, jnp.int32))

    def other_item(self, tensor):
        return exchange(tensor, "mp", self.ranks)

    def rank_pair(self, tensor):
        mask = 1
        while mask * 2 < self.ranks:
            tensor = as_low(
                tensor.astype(jnp.float32) + exchange(tensor, "mp", mask).astype(jnp.float32)
            )
            mask *= 2
        return (tensor, exchange(tensor, "mp", mask))


def gather_dp(layout, part, axis, masks):
    for mask in masks:
        part = jnp.concatenate([part, exchange(part, "dp", mask)], axis)
    return part


def gather_last_item(layout, part, axis):
    part = gather_dp(layout, part, axis, layout.masks)
    return [part, layout.other_item(part)]


def gather_last_dp(layout, part, axis):
    part = gather_dp(layout, part, axis, layout.masks[:-1])
    pair = [part, layout.other_item(part)]
    return [gather_dp(layout, half, axis, layout.masks[-1:]) for half in pair]


def add_terms(terms):
    total = terms[0].astype(jnp.float32)
    for term in terms[1:]:
        total = total + term.astype(jnp.float32)
    return total


def halve(layout, terms, mask, kind):
    half = terms[0].shape[0] // 2
    send = add_terms([term[half:] for term in terms]).astype(kind)
    return [term[:half] for term in terms] + [exchange(send, "dp", mask)]


def scatter_first_item(layout, pair):
    kind = pair[0].dtype
    terms = [pair[0], layout.other_item(pair[1])]
    for mask in reversed(layout.masks):
        terms = halve(layout, terms, mask, kind)
    return add_terms(terms)


def scatter_first_dp(layout, pair):
    kind = pair[0].dtype
    mine, theirs = [halve(layout, [part], layout.masks[-1], kind) for part in pair]
    terms = mine + [layout.other_item(add_terms(theirs).astype(kind))]
    for mask in reversed(layout.masks[:-1]):
        terms = halve(layout, terms, mask, kind)
    return add_terms(terms)


def norm_forward_kernel(parts, *refs):
    resid_ref, gain_ref = refs[0], refs[1]
    resid = resid_ref[...]
    if parts:
        resid = resid + (refs[2][...].astype(jnp.float32) + refs[3][...].astype(jnp.float32))
        refs[4][...] = resid
    centre = resid - jnp.mean(resid, -1, keepdims=True)
    inverse = lax.rsqrt(jnp.mean(centre * centre, -1, keepdims=True) + norm_eps)
    refs[-1][...] = (centre * inverse * gain_ref[...]).astype(jnp.bfloat16)


def norm_forward(resid, gain, parts=()):
    frames, width = resid.shape
    rows = min(256, frames)
    block = pl.BlockSpec((rows, width), lambda i: (i, 0))
    low_shape = jax.ShapeDtypeStruct((frames, width), jnp.bfloat16)
    result = pl.pallas_call(
        functools.partial(norm_forward_kernel, len(parts)),
        grid=(frames // rows,),
        in_specs=[block, pl.BlockSpec((1, width), lambda i: (0, 0))] + [block] * len(parts),
        out_specs=[block, block] if parts else [block],
        out_shape=[jax.ShapeDtypeStruct((frames, width), jnp.float32), low_shape]
        if parts
        else [low_shape],
        cost_estimate=pl.CostEstimate(
            flops=10 * frames * width, bytes_accessed=14 * frames * width, transcendentals=0
        ),
        compiler_params=pltpu.CompilerParams(vmem_limit_bytes=32 * 2**20),
        name="norm_fwd",
    )(resid, gain[None], *parts)
    return result if parts else (resid, result[0])


def norm_backward_kernel(has_grad, parts, *refs):
    resid_ref, gain_ref = refs[0], refs[1]
    resid = resid_ref[...]
    upstream = add_terms([ref[...] for ref in refs[2 : 2 + parts]])
    out_ref, low_ref, gain_grad_ref = refs[-3:]
    centre = resid - jnp.mean(resid, -1, keepdims=True)
    inverse = lax.rsqrt(jnp.mean(centre * centre, -1, keepdims=True) + norm_eps)
    normed = centre * inverse
    scaled = upstream * gain_ref[...]
    step = inverse * (
        scaled
        - jnp.mean(scaled, -1, keepdims=True)
        - normed * jnp.mean(scaled * normed, -1, keepdims=True)
    )
    if has_grad:
        step = refs[2 + parts][...] + step
    out_ref[...] = step
    low_ref[...] = step.astype(jnp.bfloat16)
    rows, width = resid.shape
    term = jnp.sum((upstream * normed).reshape(rows // 8, 8, width), axis=0)

    @pl.when(pl.program_id(0) == 0)
    def _():
        gain_grad_ref[...] = term

    @pl.when(pl.program_id(0) > 0)
    def _():
        gain_grad_ref[...] = gain_grad_ref[...] + term


def norm_backward(resid, gain, upstream, resid_grad=None):
    frames, width = resid.shape
    rows = min(256, frames)
    block = pl.BlockSpec((rows, width), lambda i: (i, 0))
    extra = [] if resid_grad is None else [resid_grad]
    out_grad, low_grad, gain_grad = pl.pallas_call(
        functools.partial(norm_backward_kernel, bool(extra), len(upstream)),
        grid=(frames // rows,),
        in_specs=[block, pl.BlockSpec((1, width), lambda i: (0, 0))]
        + [block] * (len(upstream) + len(extra)),
        out_specs=[block, block, pl.BlockSpec((8, width), lambda i: (0, 0))],
        out_shape=[
            jax.ShapeDtypeStruct((frames, width), jnp.float32),
            jax.ShapeDtypeStruct((frames, width), jnp.bfloat16),
            jax.ShapeDtypeStruct((8, width), jnp.float32),
        ],
        cost_estimate=pl.CostEstimate(
            flops=20 * frames * width, bytes_accessed=18 * frames * width, transcendentals=0
        ),
        compiler_params=pltpu.CompilerParams(vmem_limit_bytes=40 * 2**20),
        name="norm_bwd",
    )(resid, gain[None], *upstream, *extra)
    return (out_grad, low_grad, jnp.sum(gain_grad, 0))


def dot_nt(left, right):
    return lax.dot_general(
        left, right, (((1,), (1,)), ((), ())), preferred_element_type=jnp.float32
    )


def dot_nn(left, right):
    return jnp.dot(left, right, preferred_element_type=jnp.float32)


def head_lanes(block, head):
    lane = lax.broadcasted_iota(jnp.int32, block.shape, 1)
    keep = lane >= HEAD_DIM if head else lane < HEAD_DIM
    return jnp.where(keep, block, jnp.zeros_like(block))


def attend_forward_kernel(masked, len_ref, q_ref, k_ref, v_ref, out_ref, log_ref):
    queries, keys_in = q_ref[...], k_ref[...]
    values_t = v_ref[...].T
    outputs = []
    for head in range(2):
        scores = dot_nt(keys_in, head_lanes(queries, head))
        if masked:
            place = lax.broadcasted_iota(jnp.int32, scores.shape, 0)
            scores = jnp.where(place < len_ref[0], scores, masked_score)
        largest = jnp.max(scores, 0, keepdims=True)
        exp_scores = jnp.exp2((scores - largest) * exp_scale)
        totals = jnp.sum(exp_scores, 0, keepdims=True)
        part = dot_nn(
            values_t[head * HEAD_DIM : (head + 1) * HEAD_DIM], exp_scores.astype(jnp.bfloat16)
        )
        outputs.append(part / totals)
        log_ref[0, head : head + 1, :] = largest * exp_scale + jnp.log2(totals)
    out_ref[...] = jnp.concatenate(outputs, 0).T.astype(jnp.bfloat16)


def attend_forward(lengths, queries, q_at, keys_in, k_at, values_in, v_at, width, masked):
    frames, keys = queries.shape[0], keys_in.shape[0]
    rows = min(256, frames)
    pairs = width // LANES
    q_at, k_at, v_at = q_at // LANES, k_at // LANES, v_at // LANES
    return pl.pallas_call(
        functools.partial(attend_forward_kernel, masked),
        grid=(pairs, frames // rows),
        in_specs=[
            pl.BlockSpec(memory_space=pltpu.SMEM),
            pl.BlockSpec((rows, LANES), lambda p, i: (i, q_at + p)),
            pl.BlockSpec((keys, LANES), lambda p, i: (0, k_at + p)),
            pl.BlockSpec((keys, LANES), lambda p, i: (0, v_at + p)),
        ],
        out_specs=[
            pl.BlockSpec((rows, LANES), lambda p, i: (i, p)),
            pl.BlockSpec((1, 8, rows), lambda p, i: (p, 0, i)),
        ],
        out_shape=[
            jax.ShapeDtypeStruct((frames, width), jnp.bfloat16),
            jax.ShapeDtypeStruct((pairs, 8, frames), jnp.float32),
        ],
        cost_estimate=pl.CostEstimate(
            flops=16 * width * frames * keys,
            bytes_accessed=8 * frames * width,
            transcendentals=frames * keys * width // HEAD_DIM,
        ),
        compiler_params=pltpu.CompilerParams(vmem_limit_bytes=40 * 2**20),
        name="attend_fwd",
    )(lengths, queries, keys_in, values_in)


def attend_backward_kernel(
    masked, split, len_ref, q_ref, k_ref, v_ref, o_ref, g_ref, log_ref, *refs
):
    if split:
        dq_ref, dkv_ref, dk_acc, dv_acc, keys_t = refs
    else:
        dkv_ref, dk_acc, dv_acc, keys_t = refs
    pair, step = pl.program_id(0), pl.program_id(1)
    queries, keys_in, values_in = q_ref[...], k_ref[...], v_ref[...]
    out_grad = g_ref[...]
    rows = queries.shape[0]

    @pl.when(step == 0)
    def _():
        keys_t[...] = keys_in.T

    product = (out_grad.astype(jnp.float32) * o_ref[...].astype(jnp.float32)).T
    probs, grads, q_heads, g_heads, dq_parts = [], [], [], [], []
    for head in range(2):
        q_head, g_head = head_lanes(queries, head), head_lanes(out_grad, head)
        span = slice(head * HEAD_DIM, (head + 1) * HEAD_DIM)
        scores = dot_nt(keys_in, q_head) * exp_scale - log_ref[0, head : head + 1, :]
        if masked:
            place = lax.broadcasted_iota(jnp.int32, scores.shape, 0)
            scores = jnp.where(place < len_ref[0], scores, masked_score)
        prob = jnp.exp2(scores)
        delta = jnp.sum(product[span], 0, keepdims=True)
        grad = (prob * (dot_nt(values_in, g_head) - delta)).astype(jnp.bfloat16)
        dq_parts.append(dot_nn(keys_t[span, :], grad))
        probs.append(prob.astype(jnp.bfloat16))
        grads.append(grad)
        q_heads.append(q_head)
        g_heads.append(g_head)
    dq = (jnp.concatenate(dq_parts, 0) * score_scale).T.astype(jnp.bfloat16)
    dk = dot_nn(jnp.concatenate(grads, 1), jnp.concatenate(q_heads, 0))
    dv = dot_nn(jnp.concatenate(probs, 1), jnp.concatenate(g_heads, 0))
    width = dkv_ref.shape[1] // (2 if split else 3)
    place = pl.multiple_of(pair * LANES, LANES)
    if split:
        dq_ref[...] = dq
        k_at, v_at = place, place + width
    else:
        dkv_ref[pl.ds(pl.multiple_of(step * rows, rows), rows), pl.ds(place, LANES)] = dq
        k_at, v_at = place + width, place + 2 * width

    @pl.when(step == 0)
    def _():
        dk_acc[...] = dk
        dv_acc[...] = dv

    @pl.when(step > 0)
    def _():
        dk_acc[...] = dk_acc[...] + dk
        dv_acc[...] = dv_acc[...] + dv

    @pl.when(step == pl.num_programs(1) - 1)
    def _():
        dkv_ref[:, pl.ds(pl.multiple_of(k_at, LANES), LANES)] = (
            dk_acc[...] * score_scale
        ).astype(jnp.bfloat16)
        dkv_ref[:, pl.ds(pl.multiple_of(v_at, LANES), LANES)] = dv_acc[...].astype(jnp.bfloat16)


def attend_backward(
    lengths, queries, q_at, keys_in, k_at, values_in, v_at, outputs, out_grad, logs, width, split
):
    frames, keys = queries.shape[0], keys_in.shape[0]
    rows = min(256, frames)
    pairs = width // LANES
    q_at, k_at, v_at = q_at // LANES, k_at // LANES, v_at // LANES
    row_block = pl.BlockSpec((rows, LANES), lambda p, i: (i, p))
    outs = [jax.ShapeDtypeStruct((keys, width * (2 if split else 3)), jnp.bfloat16)]
    out_specs = [pl.BlockSpec(outs[0].shape, lambda p, i: (0, 0))]
    if split:
        outs = [jax.ShapeDtypeStruct((frames, width), jnp.bfloat16)] + outs
        out_specs = [row_block] + out_specs
    return pl.pallas_call(
        functools.partial(attend_backward_kernel, split, split),
        grid=(pairs, frames // rows),
        in_specs=[
            pl.BlockSpec(memory_space=pltpu.SMEM),
            pl.BlockSpec((rows, LANES), lambda p, i: (i, q_at + p)),
            pl.BlockSpec((keys, LANES), lambda p, i: (0, k_at + p)),
            pl.BlockSpec((keys, LANES), lambda p, i: (0, v_at + p)),
            row_block,
            row_block,
            pl.BlockSpec((1, 8, rows), lambda p, i: (p, 0, i)),
        ],
        out_specs=out_specs,
        out_shape=outs,
        scratch_shapes=[
            pltpu.VMEM((keys, LANES), jnp.float32),
            pltpu.VMEM((keys, LANES), jnp.float32),
            pltpu.VMEM((LANES, keys), jnp.bfloat16),
        ],
        cost_estimate=pl.CostEstimate(
            flops=40 * width * frames * keys,
            bytes_accessed=16 * frames * width,
            transcendentals=frames * keys * width // HEAD_DIM,
        ),
        compiler_params=pltpu.CompilerParams(vmem_limit_bytes=48 * 2**20),
        name="attend_bwd",
    )(lengths, queries, keys_in, values_in, outputs, out_grad, logs)


def frame_embedding(layout, frames, width, feature, step):
    half = width // 2
    frequency = jnp.exp(-math.log(10000.0) * (feature % half).astype(jnp.float32) / half)
    is_sin = feature < half

    def embed(position):
        angles = position[:, None] * frequency[None]
        return jnp.where(is_sin[None], jnp.sin(angles), jnp.cos(angles))

    return embed(jnp.arange(frames, dtype=jnp.float32)) + embed(step.astype(jnp.float32)[None])


def gelu_parts(hidden):
    scale = math.sqrt(2.0 / math.pi)
    square = hidden * hidden
    bend = jnp.tanh(scale * (hidden + 0.044715 * (square * hidden)))
    half_up = 0.5 * (1.0 + bend)
    slope = half_up + 0.5 * hidden * (1.0 - bend * bend) * scale * (1.0 + 3.0 * 0.044715 * square)
    return (as_low(hidden * half_up), as_low(slope))


def dot_tn(left, right):
    return lax.dot_general(
        left, right, (((0,), (0,)), ((), ())), preferred_element_type=jnp.float32
    )


def adam_update(master, first_moment, second_moment, average, gradient, factor, step_rate):
    clipped = gradient * factor
    first_new = beta_first * first_moment + (1.0 - beta_first) * clipped
    second_new = beta_second * second_moment + (1.0 - beta_second) * clipped * clipped
    first_hat = first_new / (1.0 - beta_first**STEP)
    second_hat = second_new / (1.0 - beta_second**STEP)
    master_new = master - step_rate * (
        first_hat / (jnp.sqrt(second_hat) + adam_eps) + weight_decay * master
    )
    return (
        master_new,
        first_new,
        second_new,
        average_keep * average + (1.0 - average_keep) * master_new,
    )


def local(
    latents,
    noise_draw,
    timesteps,
    text_ids,
    text_len,
    item_counts,
    text_table,
    io_weight,
    io_first,
    io_second,
    io_average,
    norm_gains,
    gains_first,
    gains_second,
    gains_average,
    col_weight,
    col_first,
    col_second,
    col_average,
    text_weight,
    text_first,
    text_second,
    text_average,
    row_weight,
    row_first,
    row_second,
    row_average,
):
    items, channels, frame_part = latents.shape
    layout = Layout(items)
    frames = frame_part * layout.mp_size
    levels, block = col_weight.shape[0], col_weight.shape[1]
    part = col_weight.shape[3]
    model_width = block * layout.dp_size
    gain_count = norm_gains.shape[0]
    text_block = text_weight.shape[1]
    item = layout.item

    col_low, row_low, text_low = as_low(col_weight), as_low(row_weight), as_low(text_weight)
    small = jnp.concatenate(
        [
            as_low(io_weight).reshape(2 * channels, block),
            as_low(norm_gains),
            jnp.full((1, block), item_counts[0], jnp.bfloat16),
        ],
        0,
    )
    small = gather_dp(layout, small[None], 0, layout.masks)
    small = jnp.swapaxes(small, 0, 1).reshape(2 * channels + gain_count + 1, model_width)
    io_w = [small[:channels], small[channels : 2 * channels]]
    gain_w = small[2 * channels : 2 * channels + gain_count].astype(jnp.float32)
    item_total = jnp.sum(small[-1].astype(jnp.float32)) / block

    qkv_w, mid_w, up_w, down_w = [], [], [], []
    text_w = None
    for level in range(levels):
        qkv_w.append(
            gather_last_item(layout, col_low[level, :, 0:3].reshape(block, 3 * part), 0)
        )
        mid_w.append(
            gather_last_dp(
                layout,
                jnp.stack([row_low[level, 0], col_low[level, :, 3], row_low[level, 1]]),
                1,
            )
        )
        if level == 0:
            text_w = gather_last_dp(
                layout, jnp.swapaxes(text_low, 0, 1).reshape(text_block, 2 * levels * part), 0
            )
        up_w.append(gather_last_item(layout, col_low[level, :, 4:].reshape(block, -1), 0))
        down_w.append(
            gather_last_dp(
                layout, jnp.swapaxes(row_low[level, 2:], 0, 1).reshape(block, -1), 0
            )
        )

    table_rows = text_table.shape[0]
    local_ids = text_ids - lax.axis_index("mp") * table_rows
    inside = (local_ids >= 0) & (local_ids < table_rows)
    picked = text_table[jnp.clip(local_ids, 0, table_rows - 1)]
    picked = jnp.where(inside[..., None], picked, jnp.zeros_like(picked))
    text_feat = lax.dynamic_index_in_dim(lax.psum(picked, "mp"), item, 0, keepdims=False)
    tokens = text_feat.shape[0]
    text_feat = jnp.take(
        text_feat.reshape(tokens, layout.dp_size, text_block), layout.blocks(), axis=1
    ).reshape(tokens, layout.dp_size * text_block)
    length = lax.dynamic_slice_in_dim(text_len, item, 1)

    steps = timesteps[item]
    alpha_bar = jnp.sum(jnp.where(steps == jnp.arange(1000), plan(), 0.0))
    alpha_all = jnp.sum(
        jnp.where(timesteps[:, None] == jnp.arange(1000)[None, :], plan()[None, :], 0.0), -1
    )
    noisy = as_low(
        jnp.sqrt(alpha_all)[:, None, None] * latents
        + jnp.sqrt(1.0 - alpha_all)[:, None, None] * noise_draw
    )
    noisy = lax.dynamic_index_in_dim(
        lax.all_gather(noisy, "mp", axis=2, tiled=True), item, 0, keepdims=False
    )
    noise = lax.dynamic_index_in_dim(
        lax.all_gather(noise_draw, "mp", axis=2, tiled=True), item, 0, keepdims=False
    )
    feature = (layout.blocks()[:, None] * block + jnp.arange(block)[None]).reshape(model_width)
    resid = dot_tn(noisy, io_w[0]) + frame_embedding(layout, frames, model_width, feature, steps)

    text_kv = [as_low(dot_nn(text_feat, weight)) for weight in text_w]

    kept_all = []
    parts = ()
    for level in range(levels):
        resid_self, normed_self = norm_forward(resid, gain_w[3 * level], parts)
        qkv = [as_low(dot_nn(normed_self, weight)) for weight in qkv_w[level]]
        attended, self_log = [], []
        for whole in qkv:
            out, log = attend_forward(
                length, whole, 0, whole, part, whole, 2 * part, part, False
            )
            attended.append(out)
            self_log.append(log)
        total = add_terms([dot_nt(o, w[0]) for o, w in zip(attended, mid_w[level])])
        parts = layout.rank_pair(as_low(total))
        resid_cross, normed_cross = norm_forward(resid_self, gain_w[3 * level + 1], parts)
        cross_query = [as_low(dot_nn(normed_cross, w[1])) for w in mid_w[level]]
        key_at = 2 * level * part
        cross_out, cross_log = [], []
        for query, text in zip(cross_query, text_kv):
            out, log = attend_forward(
                length, query, 0, text, key_at, text, key_at + part, part, True
            )
            cross_out.append(out)
            cross_log.append(log)
        total = add_terms([dot_nt(o, w[2]) for o, w in zip(cross_out, mid_w[level])])
        parts = layout.rank_pair(as_low(total))
        resid_mlp, normed_mlp = norm_forward(resid_cross, gain_w[3 * level + 2], parts)
        active, slope = [], []
        for weight in up_w[level]:
            low_value, low_slope = gelu_parts(dot_nn(normed_mlp, weight))
            active.append(low_value)
            slope.append(low_slope)
        total = add_terms([dot_nt(a, w) for a, w in zip(active, down_w[level])])
        parts = layout.rank_pair(as_low(total))
        resid = resid_mlp
        kept_all.append(
            (
                (resid_self, normed_self, qkv, attended, self_log),
                (resid_cross, normed_cross, cross_query, cross_out, cross_log),
                (resid_mlp, normed_mlp, active, slope),
            )
        )
    resid, final_low = norm_forward(resid, gain_w[3 * levels], parts)
    predicted = dot_nt(io_w[1], final_low)
    residual_error = predicted - noise
    snr_ratio = alpha_bar / (1.0 - alpha_bar)
    loss_weight = jnp.minimum(snr_ratio, snr_limit) / snr_ratio
    valid = (item < item_counts[0]).astype(jnp.float32)
    item_scale = valid * loss_weight / (channels * frames)
    loss_part = item_scale * jnp.sum(residual_error * residual_error)
    pred_grad = as_low((2.0 * item_scale / item_total) * residual_error)
    out_proj_grad = dot_nn(pred_grad, final_low)
    final_grad = dot_tn(pred_grad, io_w[1])

    gain_grads = [None] * gain_count
    resid_grad, branch_grad, gain_grads[3 * levels] = norm_backward(
        resid, gain_w[3 * levels], [final_grad]
    )
    qkv_g, mid_g, up_g, down_g = ([None] * levels for _ in range(4))
    text_grads = [[None] * levels for _ in range(items)]
    for level in reversed(range(levels)):
        kept_self, kept_cross, kept_mlp = kept_all[level]
        resid_mlp, normed_mlp, active, slope = kept_mlp
        down_g[level] = scatter_first_item(
            layout, [as_low(dot_tn(branch_grad, a)) for a in active]
        )
        hidden_grad = [
            as_low(dot_nn(branch_grad, w) * s.astype(jnp.float32))
            for w, s in zip(down_w[level], slope)
        ]
        total = add_terms([dot_nt(z, w) for z, w in zip(hidden_grad, up_w[level])])
        upstream = layout.rank_pair(as_low(total))
        up_g[level] = scatter_first_dp(
            layout, [as_low(dot_tn(normed_mlp, z)) for z in hidden_grad]
        )
        resid_grad, branch_grad, gain_grads[3 * level + 2] = norm_backward(
            resid_mlp, gain_w[3 * level + 2], upstream, resid_grad
        )

        resid_cross, normed_cross, cross_query, cross_out, cross_log = kept_cross
        key_at = 2 * level * part
        cross_w_grad, query_w_grad, query_grads = [], [], []
        for index in range(items):
            weight = mid_w[level][index]
            cross_w_grad.append(dot_tn(branch_grad, cross_out[index]))
            out_grad = as_low(dot_nn(branch_grad, weight[2]))
            text = text_kv[index]
            query_grad, text_grads[index][level] = attend_backward(
                length,
                cross_query[index],
                0,
                text,
                key_at,
                text,
                key_at + part,
                cross_out[index],
                out_grad,
                cross_log[index],
                part,
                True,
            )
            query_grads.append(query_grad)
            query_w_grad.append(dot_tn(normed_cross, query_grad))
        total = add_terms([dot_nt(q, w[1]) for q, w in zip(query_grads, mid_w[level])])
        upstream = layout.rank_pair(as_low(total))
        resid_grad, branch_grad, gain_grads[3 * level + 1] = norm_backward(
            resid_cross, gain_w[3 * level + 1], upstream, resid_grad
        )

        resid_self, normed_self, qkv, attended, self_log = kept_self
        self_w_grad, qkv_grads = [], []
        for index in range(items):
            weight, whole = mid_w[level][index], qkv[index]
            self_w_grad.append(dot_tn(branch_grad, attended[index]))
            out_grad = as_low(dot_nn(branch_grad, weight[0]))
            (grads,) = attend_backward(
                length,
                whole,
                0,
                whole,
                part,
                whole,
                2 * part,
                attended[index],
                out_grad,
                self_log[index],
                part,
                False,
            )
            qkv_grads.append(grads)
        mid_g[level] = scatter_first_item(
            layout,
            [
                as_low(jnp.concatenate(three, 1))
                for three in zip(self_w_grad, query_w_grad, cross_w_grad)
            ],
        )
        total = add_terms([dot_nt(z, w) for z, w in zip(qkv_grads, qkv_w[level])])
        upstream = layout.rank_pair(as_low(total))
        qkv_g[level] = scatter_first_dp(
            layout, [as_low(dot_tn(normed_self, z)) for z in qkv_grads]
        )
        resid_grad, branch_grad, gain_grads[3 * level] = norm_backward(
            resid_self, gain_w[3 * level], upstream, resid_grad
        )

    text_g = scatter_first_item(
        layout,
        [as_low(dot_tn(text_feat, jnp.concatenate(grads, 1))) for grads in text_grads],
    )
    in_proj_grad = dot_nn(noisy, branch_grad)
    small_grad = jnp.concatenate([in_proj_grad, out_proj_grad, jnp.stack(gain_grads)], 0)
    small_grad = small_grad.reshape(-1, layout.dp_size, block).swapaxes(0, 1)
    small_grad = scatter_first_item(layout, [small_grad, small_grad])[0]

    io_grad = small_grad[: 2 * channels].reshape(2, channels, block)
    gain_grad = small_grad[2 * channels :]
    col_grad = jnp.stack(
        [
            jnp.concatenate(
                [
                    qkv_g[level].reshape(block, 3, part),
                    mid_g[level][:, None, part : 2 * part],
                    up_g[level].reshape(block, -1, part),
                ],
                1,
            )
            for level in range(levels)
        ]
    )
    kv_grad = jnp.swapaxes(text_g.reshape(text_block, levels, 2, part), 0, 1)
    row_grad = jnp.stack(
        [
            jnp.concatenate(
                [
                    mid_g[level][None, :, :part],
                    mid_g[level][None, :, 2 * part :],
                    jnp.swapaxes(down_g[level].reshape(block, -1, part), 0, 1),
                ],
                0,
            )
            for level in range(levels)
        ]
    )

    first_owner = (lax.axis_index("mp") == 0).astype(jnp.float32)
    square = add_terms(
        [
            jnp.sum(grad * grad)
            for group in (qkv_g, mid_g, up_g, down_g, [text_g])
            for grad in group
        ]
    )
    square = square + first_owner * jnp.sum(small_grad * small_grad)
    loss_part = loss_part * (layout.rank == 0).astype(jnp.float32)
    totals = lax.psum(jnp.stack([square, loss_part]), ("dp", "mp"))
    grad_norm = jnp.sqrt(totals[0])
    factor = jnp.minimum(1.0, clip_limit / (grad_norm + 1e-06))
    results = [totals[1], item_total, grad_norm]
    io_updated = adam_update(
        io_weight, io_first, io_second, io_average, io_grad, factor, matrix_rate
    )
    results.extend(
        [io_updated[0], io_updated[1], io_updated[2][0], io_updated[2][1], io_updated[3]]
    )
    results.extend(
        adam_update(
            norm_gains, gains_first, gains_second, gains_average, gain_grad, factor, gain_rate
        )
    )
    results.extend(
        adam_update(col_weight, col_first, col_second, col_average, col_grad, factor, matrix_rate)
    )
    results.extend(
        adam_update(
            text_weight, text_first, text_second, text_average, kv_grad, factor, matrix_rate
        )
    )
    results.extend(
        adam_update(row_weight, row_first, row_second, row_average, row_grad, factor, row_rate)
    )
    return tuple(results)


def solution(mesh):
    return jax.shard_map(
        local,
        mesh=mesh,
        in_specs=(
            P("dp", None, "mp"),
            P("dp", None, "mp"),
            P("dp"),
            P("dp", None),
            P("dp"),
            P("dp"),
            P("mp", None),
            P(None, None, "dp"),
            P(None, None, "dp"),
            P(None, None, "dp"),
            P(None, None, "dp"),
            P(None, "dp"),
            P(None, "dp"),
            P(None, "dp"),
            P(None, "dp"),
            P(None, "dp", None, "mp"),
            P(None, "dp", None, "mp"),
            P(None, "dp", None, "mp"),
            P(None, "dp", None, "mp"),
            P(None, "dp", None, "mp"),
            P(None, "dp", None, "mp"),
            P(None, "dp", None, "mp"),
            P(None, "dp", None, "mp"),
            P(None, None, "dp", "mp"),
            P(None, None, "dp", "mp"),
            P(None, None, "dp", "mp"),
            P(None, None, "dp", "mp"),
        ),
        out_specs=(
            P(),
            P(),
            P(),
            P(None, None, "dp"),
            P(None, None, "dp"),
            P(None, "dp"),
            P(None, "dp"),
            P(None, None, "dp"),
            P(None, "dp"),
            P(None, "dp"),
            P(None, "dp"),
            P(None, "dp"),
            P(None, "dp", None, "mp"),
            P(None, "dp", None, "mp"),
            P(None, "dp", None, "mp"),
            P(None, "dp", None, "mp"),
            P(None, "dp", None, "mp"),
            P(None, "dp", None, "mp"),
            P(None, "dp", None, "mp"),
            P(None, "dp", None, "mp"),
            P(None, None, "dp", "mp"),
            P(None, None, "dp", "mp"),
            P(None, None, "dp", "mp"),
            P(None, None, "dp", "mp"),
        ),
        check_vma=False,
    )
```

```python
import functools
import math

import jax
import jax.numpy as jnp
from jax import lax
from jax.experimental import pallas as pl
from jax.experimental.pallas import tpu as pltpu
from jax.sharding import Mesh
from jax.sharding import PartitionSpec as P

HEAD_DIM = 64
STEP = 10
LANES = 128

QKV, MID, TEXT, UP, DOWN, SMALL = range(6)
GRAD = 10
START, DONE = range(2)
(
    AT_ATTEND,
    AT_ATTEND_NEXT,
    AT_ATTENDED,
    AT_CROSS,
    AT_CROSSED,
    AT_ACTIVE,
    AT_MLP,
    AT_HIDDEN_GRAD,
    AT_MLP_GRAD,
    AT_CROSS_GRAD,
    AT_CROSSED_GRAD,
    AT_SELF_GRAD,
    AT_SELF_GRAD_NEXT,
    AT_ATTENDED_GRAD,
) = range(14)
FULL, NEAR, ALONG_DP = range(3)
ACROSS, BESIDE, CORNER = range(100, 103)
DP, ITEM, RANK = "dp", "item", "rank"
MODEL = (ITEM, RANK)

norm_eps = 1e-06
clip_limit = 0.001
matrix_rate = 0.04
gain_rate = 0.6
row_rate = 0.1
beta_first = 0.9
beta_second = 0.999
adam_eps = 1e-08
weight_decay = 0.01
average_keep = 0.5
snr_limit = 5.0

score_scale = HEAD_DIM ** (-0.5)
log2_e = 1.4426950408889634
exp_scale = score_scale * log2_e
masked_score = -1e30


def as_low(tensor):
    return tensor.astype(jnp.bfloat16)


def plan():
    beta_table = jnp.linspace(0.00085**0.5, 0.012**0.5, 1000, dtype=jnp.float32) ** 2
    return jnp.cumprod(1.0 - beta_table)


def exchange(tensor, axis, mask):
    size = lax.axis_size(axis)
    return lax.ppermute(tensor, axis, [(i, i ^ mask) for i in range(size)])


class Layout:
    def __init__(self):
        self.dp_size = lax.axis_size(DP)
        self.items = lax.axis_size(ITEM)
        self.ranks = lax.axis_size(RANK)
        self.dp = lax.axis_index(DP)
        self.item = lax.axis_index(ITEM)
        self.rank = lax.axis_index(RANK)
        self.masks = []
        mask = self.dp_size >> 1
        while mask:
            self.masks.append(mask)
            mask >>= 1
        self.offsets = [
            sum(mask for bit, mask in enumerate(self.masks) if (place >> bit) & 1)
            for place in range(self.dp_size)
        ]

    def blocks(self):
        return jnp.bitwise_xor(self.dp, jnp.array(self.offsets, jnp.int32))

    def other_item(self, tensor):
        return exchange(tensor, ITEM, 1)


def gather_dp(layout, part, axis, masks, stages=None):
    for mask in masks:
        part = jnp.concatenate([part, exchange(part, DP, mask)], axis)
        if stages is not None:
            stages.append(part)
    return part


def nothing_kernel(*refs):
    pass


def checkpoint(values, waits):
    anywhere = pl.BlockSpec(memory_space=pl.ANY)
    return pl.pallas_call(
        nothing_kernel,
        in_specs=[anywhere] * (len(values) + len(waits)),
        out_specs=[anywhere] * len(values),
        out_shape=[jax.ShapeDtypeStruct(value.shape, value.dtype) for value in values],
        input_output_aliases={index: index for index in range(len(values))},
        cost_estimate=pl.CostEstimate(flops=0, bytes_accessed=0, transcendentals=0),
        name="checkpoint",
    )(*values, *waits)


class Gather:
    def __init__(self, layout, near, axis, first_dp, early):
        self.layout, self.near, self.axis, self.first_dp = layout, near, axis, first_dp
        self.early = early
        self.received = []

    def count(self):
        return len(self.early) + 2

    def source(self, place):
        while len(self.received) < place:
            self.send(len(self.received), self.source(len(self.received)))
        planes = place - len(self.early)
        if planes == 1:
            return self.beside if self.first_dp else self.across
        if planes < 0 and place > 0 or planes == 0 and self.early:
            self.near = jnp.concatenate([self.near, self.received[-1]], self.axis)
        return self.near

    def send(self, place, tensor):
        planes = place - len(self.early)
        if planes < 0:
            self.near = tensor
            self.received.append(exchange(tensor, DP, self.early[place]))
        elif planes == 0:
            self.near = tensor
            self.across = exchange(tensor, DP, self.layout.masks[-1])
            self.beside = self.layout.other_item(tensor)
            self.received.append((self.across, self.beside))
        else:
            if self.first_dp:
                self.beside = tensor
                self.corner = exchange(tensor, DP, self.layout.masks[-1])
            else:
                self.across = tensor
                self.corner = self.layout.other_item(tensor)
            self.received.append(self.corner)

    def finish(self):
        while len(self.received) < self.count():
            self.send(len(self.received), self.source(len(self.received)))
        return [
            jnp.concatenate([self.near, self.across], self.axis),
            jnp.concatenate([self.beside, self.corner], self.axis),
        ]


class Scatter:
    def __init__(self, layout, pair, first_dp):
        self.layout, self.first_dp, self.kind = layout, first_dp, pair[0].dtype
        half = pair[0].shape[0] // 2
        (self.near, across), (beside, self.corner) = [
            (part[:half], part[half:]) for part in pair
        ]
        self.second, self.third = (across, beside) if first_dp else (beside, across)
        self.masks = list(reversed(layout.masks[:-1]))
        self.received = []

    def count(self):
        return 3 + len(self.masks)

    def source(self, place):
        while 1 < place > len(self.received):
            self.send(len(self.received), self.source(len(self.received)))
        if place == 0:
            return self.corner
        if place == 1:
            return self.second
        if place == 2:
            return add_terms([self.third, self.received[0]]).astype(self.kind)
        if place == 3:
            self.terms = [self.near, self.received[1], self.received[2]]
        else:
            self.terms = self.terms + [self.received[-1]]
        half = self.terms[0].shape[0] // 2
        passed = add_terms([term[half:] for term in self.terms]).astype(self.kind)
        self.terms = [term[:half] for term in self.terms]
        return passed

    def send(self, place, tensor):
        if place > 2:
            moved = exchange(tensor, DP, self.masks[place - 3])
        elif self.first_dp == (place < 2):
            moved = exchange(tensor, DP, self.layout.masks[-1])
        else:
            moved = self.layout.other_item(tensor)
        self.received.append(moved)

    def finish(self):
        while len(self.received) < self.count():
            self.send(len(self.received), self.source(len(self.received)))
        return add_terms(self.terms + [self.received[-1]])


class Flow:
    def __init__(self):
        self.chunks = {}

    def add(self, name, chunk):
        self.chunks[name] = chunk
        return chunk

    def at(self, point, values):
        starts, sources, waits = [], [], []
        for action, name, level, place in flow_table.get(point, ()):
            chunk = self.chunks.get((name, level))
            if chunk is None:
                continue
            place = place if place >= 0 else chunk.count() + place
            if action == START and place >= len(chunk.received):
                starts.append((chunk, place))
                sources.append(chunk.source(place))
            elif action == DONE and place < len(chunk.received):
                got = chunk.received[place]
                waits.extend(got if isinstance(got, tuple) else [got])
        if not sources and not waits:
            return list(values)
        waits = [wait for wait in waits if all(wait is not source for source in sources)]
        result = checkpoint(list(values) + sources, waits)
        for (chunk, place), source in zip(starts, result[len(values) :]):
            chunk.send(place, source)
        return list(result[: len(values)])


class Chunk:
    def __init__(self, shape, mode, first_dp=False):
        self.shape, self.mode, self.first_dp = shape, mode, first_dp

    def out_shape(self, dp_size):
        lead = {FULL: (2, dp_size), NEAR: (dp_size // 2,), ALONG_DP: (dp_size,)}[self.mode]
        return jax.ShapeDtypeStruct(lead + self.shape, jnp.bfloat16)


def gather_order(chunks, levels):
    pending, finish = [], {}
    for index, chunk in enumerate(chunks):
        unit = chunk.shape[-1] * math.prod(chunk.shape[:-1])
        before = []
        for stage in range(levels - 1):
            cost = unit * 2**stage * (2 if stage == 0 else 1)
            pending.append((index, stage, NEAR, before, cost))
            before = before + [stage]
        block = unit * 2 ** (levels - 1)
        if chunk.mode in (FULL, ALONG_DP):
            pending.append((index, ACROSS, ACROSS, before, block))
        if chunk.mode == FULL:
            pending.append((index, BESIDE, BESIDE, before, block))
            link, need = (ACROSS, BESIDE) if chunk.first_dp else (BESIDE, ACROSS)
            pending.append((index, CORNER, link, before + [need], block))
    order, free = [], {}
    while pending:
        best = None
        for entry in pending:
            index, name, link, needs, cost = entry
            if any((index, need) not in finish for need in needs):
                continue
            ready = max([finish[index, need] for need in needs] + [0])
            start = max(free.get(link, 0), ready)
            if best is None or (start, index) < best[0]:
                best = ((start, index), entry)
        (start, _), entry = best
        index, name, link, needs, cost = entry
        free[link] = start + cost
        finish[index, name] = start + cost + 100000
        order.append(entry[:4])
        pending.remove(entry)
    return order


def gather_kernel(masks, chunks, *refs):
    count = len(chunks)
    shards, outs = refs[:count], refs[count : 2 * count]
    local_sems, send_sems, recv_sems = refs[2 * count :]
    dp, item, rank = (lax.axis_index(name) for name in (DP, ITEM, RANK))
    levels = len(masks)
    half = 2 ** (levels - 1)
    dp_peers = [{DP: jnp.bitwise_xor(dp, mask), ITEM: item, RANK: rank} for mask in masks]
    item_peer = {DP: dp, ITEM: 1 - item, RANK: rank}

    barrier = pltpu.get_barrier_semaphore()
    for peer in dp_peers + [item_peer]:
        pl.semaphore_signal(barrier, inc=1, device_id=peer, device_id_type=pl.DeviceIdType.MESH)
    pl.semaphore_wait(barrier, levels + 1)

    own = []
    for index, chunk in enumerate(chunks):
        place = outs[index].at[0, 0] if chunk.mode == FULL else outs[index].at[0]
        own.append(pltpu.make_async_copy(shards[index], place, local_sems.at[index]))
        own[-1].start()

    def transfer(index, name):
        chunk, out = chunks[index], outs[index]
        mine = out.at[0] if chunk.mode == FULL else out
        if name < ACROSS:
            stage = name
            size = 2**stage
            source, target = mine.at[pl.ds(0, size)], mine.at[pl.ds(size, size)]
            if stage == 0:
                source, target = shards[index], mine.at[1]
            return source, target, dp_peers[stage]
        if name == ACROSS:
            return mine.at[pl.ds(0, half)], mine.at[pl.ds(half, half)], dp_peers[-1]
        theirs = out.at[1]
        if name == BESIDE:
            return mine.at[pl.ds(0, half)], theirs.at[pl.ds(0, half)], item_peer
        if chunk.first_dp:
            return theirs.at[pl.ds(0, half)], theirs.at[pl.ds(half, half)], dp_peers[-1]
        return mine.at[pl.ds(half, half)], theirs.at[pl.ds(half, half)], item_peer

    copies, arrived, placed = {}, set(), set()
    for number, (index, name, _, needs) in enumerate(gather_order(chunks, levels)):
        for need in needs:
            if (index, need) not in arrived:
                arrived.add((index, need))
                copies[index, need].wait_recv()
        if needs and index not in placed:
            placed.add(index)
            own[index].wait()
        source, target, peer = transfer(index, name)
        copy = pltpu.make_async_remote_copy(
            src_ref=source,
            dst_ref=target,
            send_sem=send_sems.at[number],
            recv_sem=recv_sems.at[number],
            device_id=peer,
            device_id_type=pl.DeviceIdType.MESH,
        )
        copy.start()
        copies[index, name] = copy
    for index in range(count):
        if index not in placed:
            own[index].wait()
    for key, copy in copies.items():
        if key not in arrived:
            copy.wait_recv()
    for copy in copies.values():
        copy.wait_send()


def gather_first(layout, shards, chunks, waits):
    transfers = len(gather_order(chunks, len(layout.masks)))
    return pl.pallas_call(
        after(len(waits), functools.partial(gather_kernel, layout.masks, chunks)),
        in_specs=[pl.BlockSpec(memory_space=pl.ANY)] * (len(waits) + len(chunks)),
        out_specs=[pl.BlockSpec(memory_space=pl.ANY)] * len(chunks),
        out_shape=[chunk.out_shape(layout.dp_size) for chunk in chunks],
        scratch_shapes=[
            pltpu.SemaphoreType.DMA((len(chunks),)),
            pltpu.SemaphoreType.DMA((transfers,)),
            pltpu.SemaphoreType.DMA((transfers,)),
        ],
        compiler_params=pltpu.CompilerParams(
            collective_id=1, has_side_effects=True, vmem_limit_bytes=16 * 2**20
        ),
        cost_estimate=pl.CostEstimate(flops=10000, bytes_accessed=10**8, transcendentals=0),
        name="gather_first",
    )(*waits, *shards)


def add_terms(terms):
    total = terms[0].astype(jnp.float32)
    for term in terms[1:]:
        total = total + term.astype(jnp.float32)
    return total


def totals_kernel(value_ref, out_ref, rank_slots, dp_slots, rank_sems, dp_sems):
    dp, item, rank = (lax.axis_index(name) for name in (DP, ITEM, RANK))
    dp_size, ranks = lax.axis_size(DP), lax.axis_size(RANK)
    group = lax.axis_size(ITEM) * ranks
    me = item * ranks + rank
    group_ids, dp_ids = [], []
    for step in range(1, group):
        peer = lax.rem(me + step, group)
        group_ids.append({DP: dp, ITEM: peer // ranks, RANK: lax.rem(peer, ranks)})
    for step in range(1, dp_size):
        dp_ids.append({DP: lax.rem(dp + step, dp_size), ITEM: item, RANK: rank})
    barrier = pltpu.get_barrier_semaphore()
    for peer in group_ids + dp_ids:
        pl.semaphore_signal(barrier, inc=1, device_id=peer, device_id_type=pl.DeviceIdType.MESH)
    pl.semaphore_wait(barrier, len(group_ids) + len(dp_ids))

    def share(place, slots, sems, peers):
        copies = []
        for step, peer in enumerate(peers):
            copies.append(
                pltpu.make_async_remote_copy(
                    src_ref=slots.at[place],
                    dst_ref=slots.at[place],
                    send_sem=sems.at[0, step],
                    recv_sem=sems.at[1, step],
                    device_id=peer,
                    device_id_type=pl.DeviceIdType.MESH,
                )
            )
            copies[-1].start()
        for copy in copies:
            copy.wait()
        total = slots[0]
        for index in range(1, len(peers) + 1):
            total = total + slots[index]
        return total

    rank_slots[me] = value_ref[...]
    dp_slots[dp] = share(me, rank_slots, rank_sems, group_ids)
    out_ref[...] = share(dp, dp_slots, dp_sems, dp_ids)


def all_totals(layout, values):
    tile = jnp.zeros((8, LANES), jnp.float32).at[0, : values.shape[0]].set(values)
    group = layout.items * layout.ranks
    total = pl.pallas_call(
        totals_kernel,
        in_specs=[pl.BlockSpec(memory_space=pltpu.VMEM)],
        out_specs=pl.BlockSpec(memory_space=pltpu.VMEM),
        out_shape=jax.ShapeDtypeStruct(tile.shape, jnp.float32),
        scratch_shapes=[
            pltpu.VMEM((group,) + tile.shape, jnp.float32),
            pltpu.VMEM((layout.dp_size,) + tile.shape, jnp.float32),
            pltpu.SemaphoreType.DMA((2, group - 1)),
            pltpu.SemaphoreType.DMA((2, layout.dp_size - 1)),
        ],
        compiler_params=pltpu.CompilerParams(collective_id=0, has_side_effects=True),
        cost_estimate=pl.CostEstimate(flops=10000, bytes_accessed=100000, transcendentals=0),
        name="totals",
    )(tile)
    return total[0, : values.shape[0]]


def swapped_sum(part_ref, own_ref, slots, send_sems, recv_sems):
    ranks = lax.axis_size(RANK)
    dp, item, rank = (lax.axis_index(name) for name in (DP, ITEM, RANK))
    step, steps = pl.program_id(0), part_ref.shape[0] // own_ref.shape[0]
    rows = own_ref.shape[0]
    place = 0 if ranks == 2 else rank
    peers = [
        {DP: dp, ITEM: item, RANK: lax.rem(rank + ahead, ranks)} for ahead in range(1, ranks)
    ]

    def copies(chunk):
        span = pl.ds(pl.multiple_of(chunk * rows, rows), rows)
        return [
            pltpu.make_async_remote_copy(
                src_ref=part_ref.at[span],
                dst_ref=slots.at[place, span],
                send_sem=send_sems.at[index, chunk],
                recv_sem=recv_sems.at[index, chunk],
                device_id=peer,
                device_id_type=pl.DeviceIdType.MESH,
            )
            for index, peer in enumerate(peers)
        ]

    @pl.when(step == 0)
    def _():
        barrier = pltpu.get_barrier_semaphore()
        for peer in peers:
            pl.semaphore_signal(
                barrier, inc=1, device_id=peer, device_id_type=pl.DeviceIdType.MESH
            )
        pl.semaphore_wait(barrier, len(peers))
        for chunk in range(steps):
            for copy in copies(chunk):
                copy.start()

    for copy in copies(step):
        copy.wait_recv()
    span = pl.ds(pl.multiple_of(step * rows, rows), rows)
    if ranks == 2:
        total = own_ref[...].astype(jnp.float32) + slots[0, span].astype(jnp.float32)
    else:
        slots[rank, span] = own_ref[...]
        total = add_terms([slots[index, span] for index in range(ranks)])

    @pl.when(step == steps - 1)
    def _():
        for chunk in range(steps):
            for copy in copies(chunk):
                copy.wait_send()

    return total


def swap_scratch(ranks, frames, rows, width):
    return [
        pltpu.VMEM((1 if ranks == 2 else ranks, frames, width), jnp.bfloat16),
        pltpu.SemaphoreType.DMA((ranks - 1, frames // rows)),
        pltpu.SemaphoreType.DMA((ranks - 1, frames // rows)),
    ]


def normalise(resid):
    centre = resid - jnp.mean(resid, -1, keepdims=True)
    inverse = lax.rsqrt(jnp.mean(centre * centre, -1, keepdims=True) + norm_eps)
    return (centre * inverse, inverse)


def norm_forward_kernel(resid_ref, gain_ref, low_ref):
    low_ref[...] = (normalise(resid_ref[...])[0] * gain_ref[...]).astype(jnp.bfloat16)


def norm_swap_forward_kernel(part_ref, own_ref, resid_ref, gain_ref, out_ref, low_ref, *swap):
    resid = resid_ref[...] + swapped_sum(part_ref, own_ref, *swap)
    out_ref[...] = resid
    low_ref[...] = (normalise(resid)[0] * gain_ref[...]).astype(jnp.bfloat16)


def norm_forward(resid, gain, part=None):
    frames, width = resid.shape
    rows = min(256, frames)
    block = pl.BlockSpec((rows, width), lambda i: (i, 0))
    gain_block = pl.BlockSpec((1, width), lambda i: (0, 0))
    low_shape = jax.ShapeDtypeStruct((frames, width), jnp.bfloat16)
    cost = pl.CostEstimate(
        flops=10 * frames * width, bytes_accessed=14 * frames * width, transcendentals=0
    )
    if part is None:
        return (
            resid,
            pl.pallas_call(
                norm_forward_kernel,
                grid=(frames // rows,),
                in_specs=[block, gain_block],
                out_specs=block,
                out_shape=low_shape,
                cost_estimate=cost,
                compiler_params=pltpu.CompilerParams(vmem_limit_bytes=32 * 2**20),
                name="norm_fwd",
            )(resid, gain[None]),
        )
    return pl.pallas_call(
        norm_swap_forward_kernel,
        grid=(frames // rows,),
        in_specs=[pl.BlockSpec(memory_space=pl.ANY), block, block, gain_block],
        out_specs=[block, block],
        out_shape=[jax.ShapeDtypeStruct((frames, width), jnp.float32), low_shape],
        scratch_shapes=swap_scratch(lax.axis_size(RANK), frames, rows, width),
        cost_estimate=cost,
        compiler_params=pltpu.CompilerParams(
            collective_id=2, has_side_effects=True, vmem_limit_bytes=32 * 2**20
        ),
        name="norm_swap_fwd",
    )(part, part, resid, gain[None])


def norm_step(resid, gain, upstream):
    normed, inverse = normalise(resid)
    scaled = upstream * gain
    step = inverse * (
        scaled
        - jnp.mean(scaled, -1, keepdims=True)
        - normed * jnp.mean(scaled * normed, -1, keepdims=True)
    )
    rows, width = resid.shape
    return (step, jnp.sum((upstream * normed).reshape(rows // 8, 8, width), axis=0))


def add_gain_term(gain_grad_ref, term):
    @pl.when(pl.program_id(0) == 0)
    def _():
        gain_grad_ref[...] = term

    @pl.when(pl.program_id(0) > 0)
    def _():
        gain_grad_ref[...] = gain_grad_ref[...] + term


def norm_backward_kernel(upstream_ref, resid_ref, gain_ref, out_ref, low_ref, gain_grad_ref):
    step, term = norm_step(resid_ref[...], gain_ref[...], upstream_ref[...])
    out_ref[...] = step
    low_ref[...] = step.astype(jnp.bfloat16)
    add_gain_term(gain_grad_ref, term)


def norm_swap_backward_kernel(
    part_ref, own_ref, resid_ref, gain_ref, grad_ref, out_ref, low_ref, gain_grad_ref, *swap
):
    upstream = swapped_sum(part_ref, own_ref, *swap)
    step, term = norm_step(resid_ref[...], gain_ref[...], upstream)
    step = grad_ref[...] + step
    out_ref[...] = step
    low_ref[...] = step.astype(jnp.bfloat16)
    add_gain_term(gain_grad_ref, term)


def norm_backward(resid, gain, upstream, resid_grad=None, waits=()):
    frames, width = resid.shape
    rows = min(256, frames)
    block = pl.BlockSpec((rows, width), lambda i: (i, 0))
    gain_block = pl.BlockSpec((1, width), lambda i: (0, 0))
    out_specs = [block, block, pl.BlockSpec((8, width), lambda i: (0, 0))]
    out_shape = [
        jax.ShapeDtypeStruct((frames, width), jnp.float32),
        jax.ShapeDtypeStruct((frames, width), jnp.bfloat16),
        jax.ShapeDtypeStruct((8, width), jnp.float32),
    ]
    cost = pl.CostEstimate(
        flops=20 * frames * width, bytes_accessed=18 * frames * width, transcendentals=0
    )
    if resid_grad is None:
        result = pl.pallas_call(
            norm_backward_kernel,
            grid=(frames // rows,),
            in_specs=[block, block, gain_block],
            out_specs=out_specs,
            out_shape=out_shape,
            cost_estimate=cost,
            compiler_params=pltpu.CompilerParams(vmem_limit_bytes=40 * 2**20),
            name="norm_bwd",
        )(upstream, resid, gain[None])
    else:
        result = pl.pallas_call(
            after(len(waits), norm_swap_backward_kernel),
            grid=(frames // rows,),
            in_specs=[pl.BlockSpec(memory_space=pl.ANY)] * (len(waits) + 1)
            + [block, block, gain_block, block],
            out_specs=out_specs,
            out_shape=out_shape,
            scratch_shapes=swap_scratch(lax.axis_size(RANK), frames, rows, width),
            cost_estimate=cost,
            compiler_params=pltpu.CompilerParams(
                collective_id=4 if waits else 3, has_side_effects=True, vmem_limit_bytes=40 * 2**20
            ),
            name="norm_swap_bwd",
        )(*waits, upstream, upstream, resid, gain[None], resid_grad)
    return (result[0], result[1], jnp.sum(result[2], 0))


def after(count, kernel):
    return lambda *refs: kernel(*refs[count:])


def dot_nt(left, right):
    return lax.dot_general(
        left, right, (((1,), (1,)), ((), ())), preferred_element_type=jnp.float32
    )


def dot_nn(left, right):
    return jnp.dot(left, right, preferred_element_type=jnp.float32)


def head_lanes(block, head):
    lane = lax.broadcasted_iota(jnp.int32, block.shape, 1)
    keep = lane >= HEAD_DIM if head else lane < HEAD_DIM
    return jnp.where(keep, block, jnp.zeros_like(block))


def attend_forward_kernel(masked, len_ref, q_ref, k_ref, v_ref, out_ref, log_ref):
    queries, keys_in = q_ref[...], k_ref[...]
    values_t = v_ref[...].T
    outputs = []
    for head in range(2):
        scores = dot_nt(keys_in, head_lanes(queries, head))
        if masked:
            place = lax.broadcasted_iota(jnp.int32, scores.shape, 0)
            scores = jnp.where(place < len_ref[0], scores, masked_score)
        largest = jnp.max(scores, 0, keepdims=True)
        exp_scores = jnp.exp2((scores - largest) * exp_scale)
        totals = jnp.sum(exp_scores, 0, keepdims=True)
        part = dot_nn(
            values_t[head * HEAD_DIM : (head + 1) * HEAD_DIM], exp_scores.astype(jnp.bfloat16)
        )
        outputs.append(part / totals)
        log_ref[0, head : head + 1, :] = largest * exp_scale + jnp.log2(totals)
    out_ref[...] = jnp.concatenate(outputs, 0).T.astype(jnp.bfloat16)


def attend_forward(lengths, queries, q_at, keys_in, k_at, values_in, v_at, width, masked, waits=()):
    frames, keys = queries.shape[0], keys_in.shape[0]
    rows = min(256, frames)
    pairs = width // LANES
    q_at, k_at, v_at = q_at // LANES, k_at // LANES, v_at // LANES
    return pl.pallas_call(
        after(len(waits), functools.partial(attend_forward_kernel, masked)),
        grid=(pairs, frames // rows),
        in_specs=[pl.BlockSpec(memory_space=pl.ANY)] * len(waits)
        + [
            pl.BlockSpec(memory_space=pltpu.SMEM),
            pl.BlockSpec((rows, LANES), lambda p, i: (i, q_at + p)),
            pl.BlockSpec((keys, LANES), lambda p, i: (0, k_at + p)),
            pl.BlockSpec((keys, LANES), lambda p, i: (0, v_at + p)),
        ],
        out_specs=[
            pl.BlockSpec((rows, LANES), lambda p, i: (i, p)),
            pl.BlockSpec((1, 8, rows), lambda p, i: (p, 0, i)),
        ],
        out_shape=[
            jax.ShapeDtypeStruct((frames, width), jnp.bfloat16),
            jax.ShapeDtypeStruct((pairs, 8, frames), jnp.float32),
        ],
        cost_estimate=pl.CostEstimate(
            flops=16 * width * frames * keys,
            bytes_accessed=8 * frames * width,
            transcendentals=frames * keys * width // HEAD_DIM,
        ),
        compiler_params=pltpu.CompilerParams(vmem_limit_bytes=40 * 2**20),
        name="attend_fwd",
    )(*waits, lengths, queries, keys_in, values_in)


def attend_backward_kernel(
    masked, split, len_ref, q_ref, k_ref, v_ref, o_ref, g_ref, log_ref, *refs
):
    if split:
        dq_ref, dkv_ref, dk_acc, dv_acc, keys_t = refs
    else:
        dkv_ref, dk_acc, dv_acc, keys_t = refs
    pair, step = pl.program_id(0), pl.program_id(1)
    queries, keys_in, values_in = q_ref[...], k_ref[...], v_ref[...]
    out_grad = g_ref[...]
    rows = queries.shape[0]

    @pl.when(step == 0)
    def _():
        keys_t[...] = keys_in.T

    product = (out_grad.astype(jnp.float32) * o_ref[...].astype(jnp.float32)).T
    probs, grads, q_heads, g_heads, dq_parts = [], [], [], [], []
    for head in range(2):
        q_head, g_head = head_lanes(queries, head), head_lanes(out_grad, head)
        span = slice(head * HEAD_DIM, (head + 1) * HEAD_DIM)
        scores = dot_nt(keys_in, q_head) * exp_scale - log_ref[0, head : head + 1, :]
        if masked:
            place = lax.broadcasted_iota(jnp.int32, scores.shape, 0)
            scores = jnp.where(place < len_ref[0], scores, masked_score)
        prob = jnp.exp2(scores)
        delta = jnp.sum(product[span], 0, keepdims=True)
        grad = (prob * (dot_nt(values_in, g_head) - delta)).astype(jnp.bfloat16)
        dq_parts.append(dot_nn(keys_t[span, :], grad))
        probs.append(prob.astype(jnp.bfloat16))
        grads.append(grad)
        q_heads.append(q_head)
        g_heads.append(g_head)
    dq = (jnp.concatenate(dq_parts, 0) * score_scale).T.astype(jnp.bfloat16)
    dk = dot_nn(jnp.concatenate(grads, 1), jnp.concatenate(q_heads, 0))
    dv = dot_nn(jnp.concatenate(probs, 1), jnp.concatenate(g_heads, 0))
    width = dkv_ref.shape[1] // (2 if split else 3)
    place = pl.multiple_of(pair * LANES, LANES)
    if split:
        dq_ref[...] = dq
        k_at, v_at = place, place + width
    else:
        dkv_ref[pl.ds(pl.multiple_of(step * rows, rows), rows), pl.ds(place, LANES)] = dq
        k_at, v_at = place + width, place + 2 * width

    @pl.when(step == 0)
    def _():
        dk_acc[...] = dk
        dv_acc[...] = dv

    @pl.when(step > 0)
    def _():
        dk_acc[...] = dk_acc[...] + dk
        dv_acc[...] = dv_acc[...] + dv

    @pl.when(step == pl.num_programs(1) - 1)
    def _():
        dkv_ref[:, pl.ds(pl.multiple_of(k_at, LANES), LANES)] = (
            dk_acc[...] * score_scale
        ).astype(jnp.bfloat16)
        dkv_ref[:, pl.ds(pl.multiple_of(v_at, LANES), LANES)] = dv_acc[...].astype(jnp.bfloat16)


def attend_backward(
    lengths, queries, q_at, keys_in, k_at, values_in, v_at, outputs, out_grad, logs, width, split, waits=()
):
    frames, keys = queries.shape[0], keys_in.shape[0]
    rows = min(256, frames)
    pairs = width // LANES
    q_at, k_at, v_at = q_at // LANES, k_at // LANES, v_at // LANES
    row_block = pl.BlockSpec((rows, LANES), lambda p, i: (i, p))
    outs = [jax.ShapeDtypeStruct((keys, width * (2 if split else 3)), jnp.bfloat16)]
    out_specs = [pl.BlockSpec(outs[0].shape, lambda p, i: (0, 0))]
    if split:
        outs = [jax.ShapeDtypeStruct((frames, width), jnp.bfloat16)] + outs
        out_specs = [row_block] + out_specs
    return pl.pallas_call(
        after(len(waits), functools.partial(attend_backward_kernel, split, split)),
        grid=(pairs, frames // rows),
        in_specs=[pl.BlockSpec(memory_space=pl.ANY)] * len(waits)
        + [
            pl.BlockSpec(memory_space=pltpu.SMEM),
            pl.BlockSpec((rows, LANES), lambda p, i: (i, q_at + p)),
            pl.BlockSpec((keys, LANES), lambda p, i: (0, k_at + p)),
            pl.BlockSpec((keys, LANES), lambda p, i: (0, v_at + p)),
            row_block,
            row_block,
            pl.BlockSpec((1, 8, rows), lambda p, i: (p, 0, i)),
        ],
        out_specs=out_specs,
        out_shape=outs,
        scratch_shapes=[
            pltpu.VMEM((keys, LANES), jnp.float32),
            pltpu.VMEM((keys, LANES), jnp.float32),
            pltpu.VMEM((LANES, keys), jnp.bfloat16),
        ],
        cost_estimate=pl.CostEstimate(
            flops=40 * width * frames * keys,
            bytes_accessed=16 * frames * width,
            transcendentals=frames * keys * width // HEAD_DIM,
        ),
        compiler_params=pltpu.CompilerParams(vmem_limit_bytes=48 * 2**20),
        name="attend_bwd",
    )(*waits, lengths, queries, keys_in, values_in, outputs, out_grad, logs)


flow_table = {
    (AT_ATTENDED, 0): [
        (DONE, UP, 0, 0),
        (DONE, DOWN, 0, 0),
        (DONE, UP, 1, 0),
        (DONE, DOWN, 1, 0),
        (START, UP, 0, 1),
        (START, DOWN, 0, 1),
        (START, UP, 1, 1),
        (START, DOWN, 1, 1),
    ],
    (AT_CROSSED, 0): [
        (DONE, UP, 0, 1),
        (DONE, DOWN, 0, 1),
        (DONE, UP, 1, 1),
        (DONE, DOWN, 1, 1),
        (START, QKV, 1, 0),
        (START, MID, 1, 0),
    ],
    (AT_MLP, 0): [
        (DONE, QKV, 1, 0),
        (DONE, MID, 1, 0),
        (START, QKV, 1, 1),
        (START, MID, 1, 1),
    ],
    (AT_ATTEND, 1): [
        (DONE, MID, 1, 1),
        (START, UP, 1, 2),
        (START, DOWN, 1, 2),
    ],
    (AT_CROSS, 1): [
        (DONE, UP, 1, 2),
        (DONE, DOWN, 1, 2),
        (START, UP, 1, 3),
        (START, DOWN, 1, 3),
    ],
    (AT_HIDDEN_GRAD, 1): [(START, GRAD + DOWN, 1, 0)],
    (AT_MLP_GRAD, 1): [(START, GRAD + DOWN, 1, 1), (START, GRAD + UP, 1, 0)],
    (AT_CROSS_GRAD, 1): [
        (DONE, GRAD + DOWN, 1, 0),
        (START, GRAD + DOWN, 1, 2),
        (START, GRAD + UP, 1, 1),
    ],
    (AT_CROSSED_GRAD, 1): [
        (DONE, GRAD + DOWN, 1, 1),
        (DONE, GRAD + UP, 1, 0),
        (START, GRAD + UP, 1, 2),
    ],
    (AT_SELF_GRAD, 1): [(DONE, GRAD + UP, 1, 1), (START, GRAD + MID, 1, 0)],
    (AT_SELF_GRAD_NEXT, 1): [
        (DONE, GRAD + DOWN, 1, 2),
        (DONE, GRAD + UP, 1, 2),
        (START, GRAD + DOWN, 1, 3),
        (START, GRAD + UP, 1, 3),
        (START, GRAD + MID, 1, 1),
    ],
    (AT_ATTENDED_GRAD, 1): [
        (DONE, GRAD + MID, 1, 0),
        (DONE, GRAD + MID, 1, 1),
        (START, GRAD + MID, 1, 2),
        (START, GRAD + QKV, 1, 0),
    ],
    (AT_HIDDEN_GRAD, 0): [
        (DONE, GRAD + DOWN, 1, 3),
        (DONE, GRAD + UP, 1, 3),
        (START, GRAD + DOWN, 0, 0),
        (START, GRAD + QKV, 1, 1),
        (START, GRAD + DOWN, 1, 4),
        (START, GRAD + UP, 1, 4),
    ],
    (AT_MLP_GRAD, 0): [
        (DONE, GRAD + MID, 1, 2),
        (DONE, GRAD + QKV, 1, 0),
        (START, GRAD + QKV, 1, 2),
        (START, GRAD + DOWN, 0, 1),
        (START, GRAD + MID, 1, 3),
    ],
    (AT_CROSS_GRAD, 0): [
        (DONE, GRAD + DOWN, 0, 0),
        (DONE, GRAD + QKV, 1, 1),
        (START, GRAD + UP, 0, 0),
        (DONE, GRAD + DOWN, 1, 4),
        (DONE, GRAD + UP, 1, 4),
    ],
    (AT_CROSSED_GRAD, 0): [
        (DONE, GRAD + DOWN, 0, 1),
        (DONE, GRAD + QKV, 1, 2),
        (DONE, GRAD + MID, 1, 3),
        (START, GRAD + DOWN, 0, 2),
        (START, GRAD + UP, 0, 1),
        (START, GRAD + QKV, 1, 3),
        (START, GRAD + MID, 1, 4),
    ],
    (AT_SELF_GRAD, 0): [
        (DONE, GRAD + UP, 0, 0),
        (START, GRAD + UP, 0, 2),
        (START, GRAD + MID, 0, 0),
        (START, GRAD + TEXT, 0, 0),
    ],
    (AT_SELF_GRAD_NEXT, 0): [
        (DONE, GRAD + DOWN, 0, 2),
        (DONE, GRAD + UP, 0, 1),
        (DONE, GRAD + QKV, 1, 3),
        (DONE, GRAD + MID, 1, 4),
        (START, GRAD + DOWN, 0, 3),
        (START, GRAD + MID, 0, 1),
        (START, GRAD + TEXT, 0, 1),
        (START, GRAD + QKV, 1, 4),
    ],
    (AT_ATTENDED_GRAD, 0): [
        (DONE, GRAD + UP, 0, 2),
        (DONE, GRAD + MID, 0, 0),
        (DONE, GRAD + TEXT, 0, 0),
        (DONE, GRAD + DOWN, 0, 3),
        (START, GRAD + QKV, 0, 0),
        (START, GRAD + QKV, 0, 1),
        (START, GRAD + MID, 0, 2),
        (START, GRAD + TEXT, 0, 2),
        (START, GRAD + UP, 0, 3),
        (START, GRAD + DOWN, 0, 4),
    ],
}
first_modes = {
    (SMALL, 0): ALONG_DP,
    (QKV, 0): FULL,
    (MID, 0): FULL,
    (TEXT, 0): FULL,
    (UP, 0): NEAR,
    (DOWN, 0): NEAR,
    (QKV, 1): NEAR,
    (MID, 1): NEAR,
}


def frame_embedding(frames, feature, width, step):
    half = width // 2
    frequency = jnp.exp(-math.log(10000.0) * (feature % half).astype(jnp.float32) / half)
    is_sin = (feature < half)[None]
    span = min(32, frames)

    def turns(position):
        angles = position.astype(jnp.float32)[:, None] * frequency
        return (jnp.sin(angles), jnp.cos(angles))

    sin_high, cos_high = turns(jnp.arange(frames // span) * span)
    sin_low, cos_low = turns(jnp.arange(span))
    sin_step, cos_step = turns(step[None])
    times_cos = jnp.where(is_sin, sin_high, cos_high)[:, None]
    times_sin = jnp.where(is_sin, cos_high, -sin_high)[:, None]
    table = times_cos * cos_low[None] + times_sin * sin_low[None]
    return table.reshape(frames, width) + jnp.where(is_sin, sin_step, cos_step)


def gelu_parts(hidden):
    scale = math.sqrt(2.0 / math.pi)
    square = hidden * hidden
    bend = jnp.tanh(scale * (hidden + 0.044715 * (square * hidden)))
    half_up = 0.5 * (1.0 + bend)
    slope = half_up + 0.5 * hidden * (1.0 - bend * bend) * scale * (1.0 + 3.0 * 0.044715 * square)
    return (as_low(hidden * half_up), as_low(slope))


def dot_tn(left, right):
    return lax.dot_general(
        left, right, (((0,), (0,)), ((), ())), preferred_element_type=jnp.float32
    )


def adam_update(master, first_moment, second_moment, average, gradient, factor, step_rate):
    clipped = gradient * factor
    first_new = beta_first * first_moment + (1.0 - beta_first) * clipped
    second_new = beta_second * second_moment + (1.0 - beta_second) * clipped * clipped
    first_hat = first_new / (1.0 - beta_first**STEP)
    second_hat = second_new / (1.0 - beta_second**STEP)
    master_new = master - step_rate * (
        first_hat / (jnp.sqrt(second_hat) + adam_eps) + weight_decay * master
    )
    return (
        master_new,
        first_new,
        second_new,
        average_keep * average + (1.0 - average_keep) * master_new,
    )


def local(
    latents,
    noise_draw,
    timesteps,
    text_ids,
    text_len,
    item_counts,
    text_table,
    io_weight,
    io_first,
    io_second,
    io_average,
    norm_gains,
    gains_first,
    gains_second,
    gains_average,
    col_weight,
    col_first,
    col_second,
    col_average,
    text_weight,
    text_first,
    text_second,
    text_average,
    row_weight,
    row_first,
    row_second,
    row_average,
):
    items, channels, frame_part = latents.shape
    layout = Layout()
    group = layout.items * layout.ranks
    frames = frame_part * group
    levels, block = col_weight.shape[0], col_weight.shape[1]
    part = col_weight.shape[3]
    model_width = block * layout.dp_size
    gain_count = norm_gains.shape[0]
    text_block = text_weight.shape[1]
    item = layout.item

    table_rows = text_table.shape[0]
    local_ids = text_ids - (item * layout.ranks + layout.rank) * table_rows
    inside = (local_ids >= 0) & (local_ids < table_rows)
    picked = text_table[jnp.clip(local_ids, 0, table_rows - 1)]
    picked = jnp.where(inside[..., None], picked, jnp.zeros_like(picked))
    length = lax.dynamic_slice_in_dim(text_len, item, 1)

    steps = timesteps[item]
    alpha_bar = jnp.sum(jnp.where(steps == jnp.arange(1000), plan(), 0.0))
    alpha_all = jnp.sum(
        jnp.where(timesteps[:, None] == jnp.arange(1000)[None, :], plan()[None, :], 0.0), -1
    )
    noisy = (
        jnp.sqrt(alpha_all)[:, None, None] * latents
        + jnp.sqrt(1.0 - alpha_all)[:, None, None] * noise_draw
    )
    frames_all = lax.all_gather(
        jnp.concatenate([noisy, noise_draw], 1), MODEL, axis=2, tiled=True
    )
    frames_all = lax.dynamic_index_in_dim(frames_all, item, 0, keepdims=False)
    noisy, noise = as_low(frames_all[:channels]), frames_all[channels:]
    feature = (layout.blocks()[:, None] * block + jnp.arange(block)[None]).reshape(model_width)
    embedding = frame_embedding(frames, feature, model_width, steps)

    col_low, row_low, text_low = as_low(col_weight), as_low(row_weight), as_low(text_weight)
    small = jnp.concatenate(
        [
            as_low(io_weight).reshape(2 * channels, block),
            as_low(norm_gains),
            jnp.full((1, block), item_counts[0], jnp.bfloat16),
        ],
        0,
    )
    shards = {
        (SMALL, 0): small,
        (TEXT, 0): jnp.swapaxes(text_low, 0, 1).reshape(text_block, 2 * levels * part),
    }
    for level in range(levels):
        shards[QKV, level] = col_low[level, :, 0:3].reshape(block, 3 * part)
        shards[MID, level] = jnp.stack(
            [row_low[level, 0], col_low[level, :, 3], row_low[level, 1]]
        )
        shards[UP, level] = col_low[level, :, 4:].reshape(block, -1)
        shards[DOWN, level] = jnp.swapaxes(row_low[level, 2:], 0, 1).reshape(block, -1)
    names = [(SMALL, 0), (QKV, 0), (MID, 0), (TEXT, 0), (UP, 0), (DOWN, 0)]
    for level in range(1, levels):
        names += [(QKV, level), (MID, level), (UP, level), (DOWN, level)]
    kernel_names = [name for name in names if name in first_modes]
    chunks = [
        Chunk(shards[name].shape, first_modes[name], names.index(name) % 2 == 0)
        for name in kernel_names
    ]
    gathered = dict(
        zip(
            kernel_names,
            gather_first(
                layout,
                [shards[name] for name in kernel_names],
                chunks,
                [noisy, noise, embedding, picked],
            ),
        )
    )
    flow = Flow()
    weights = {}
    for name in names[1:]:
        axis = 1 if name[0] == MID else 0
        if first_modes.get(name) == FULL:
            pair = [gathered[name][index] for index in range(items)]
            if axis == 1:
                weights[name] = [
                    [half[:, index].reshape(model_width, part) for index in range(3)]
                    for half in pair
                ]
            else:
                weights[name] = [half.reshape((-1,) + half.shape[2:]) for half in pair]
            continue
        near, early = shards[name], layout.masks[:-1]
        if name in gathered:
            near, early = gathered[name], []
            near = near.reshape((-1,) + near.shape[2:]) if axis == 0 else near.swapaxes(0, 1)
        near = near.reshape((3, -1, part)) if axis == 1 else near
        flow.add(name, Gather(layout, near, axis, names.index(name) % 2 == 0, early))
    for name, chunk in flow.chunks.items():
        if name[1] == 0 or chunk.early:
            chunk.send(0, chunk.source(0))

    def weight(name, level):
        if (name, level) not in weights:
            weights[name, level] = flow.chunks[name, level].finish()
        return weights[name, level]

    small = jnp.swapaxes(gathered[SMALL, 0], 0, 1)
    small = small.reshape(2 * channels + gain_count + 1, model_width)
    io_w = [small[:channels], small[channels : 2 * channels]]
    gain_w = small[2 * channels : 2 * channels + gain_count].astype(jnp.float32)
    item_total = jnp.sum(small[-1].astype(jnp.float32)) / block
    text_w = weights[TEXT, 0]

    text_feat = lax.dynamic_index_in_dim(lax.psum(picked, MODEL), item, 0, keepdims=False)
    tokens = text_feat.shape[0]
    text_feat = jnp.take(
        text_feat.reshape(tokens, layout.dp_size, text_block), layout.blocks(), axis=1
    ).reshape(tokens, layout.dp_size * text_block)
    resid = dot_tn(noisy, io_w[0]) + embedding

    text_kv = [as_low(dot_nn(text_feat, weight)) for weight in text_w]

    kept_all = []
    part_sum = None
    for level in range(levels):
        resid_self, normed_self = norm_forward(resid, gain_w[3 * level], part_sum)
        qkv = [as_low(dot_nn(normed_self, w)) for w in weight(QKV, level)]
        qkv = flow.at((AT_ATTEND, level), qkv)
        attended, self_log = [None] * items, [None] * items
        for index in range(items):
            if index:
                qkv[index:] = flow.at((AT_ATTEND_NEXT, level), qkv[index:])
            whole = qkv[index]
            attended[index], self_log[index] = attend_forward(
                length, whole, 0, whole, part, whole, 2 * part, part, False
            )
        total = add_terms([dot_nt(o, w[0]) for o, w in zip(attended, weight(MID, level))])
        (part_sum,) = flow.at((AT_ATTENDED, level), [as_low(total)])
        resid_cross, normed_cross = norm_forward(resid_self, gain_w[3 * level + 1], part_sum)
        cross_query = [as_low(dot_nn(normed_cross, w[1])) for w in weight(MID, level)]
        cross_query = flow.at((AT_CROSS, level), cross_query)
        key_at = 2 * level * part
        cross_out, cross_log = [], []
        for query, text in zip(cross_query, text_kv):
            out, log = attend_forward(
                length, query, 0, text, key_at, text, key_at + part, part, True
            )
            cross_out.append(out)
            cross_log.append(log)
        total = add_terms([dot_nt(o, w[2]) for o, w in zip(cross_out, weight(MID, level))])
        (part_sum,) = flow.at((AT_CROSSED, level), [as_low(total)])
        resid_mlp, normed_mlp = norm_forward(resid_cross, gain_w[3 * level + 2], part_sum)
        active, slope = [], []
        for w in weight(UP, level):
            low_value, low_slope = gelu_parts(dot_nn(normed_mlp, w))
            active.append(low_value)
            slope.append(low_slope)
        active = flow.at((AT_ACTIVE, level), active)
        total = add_terms([dot_nt(a, w) for a, w in zip(active, weight(DOWN, level))])
        (part_sum,) = flow.at((AT_MLP, level), [as_low(total)])
        resid = resid_mlp
        kept_all.append(
            (
                (resid_self, normed_self, qkv, attended, self_log),
                (resid_cross, normed_cross, cross_query, cross_out, cross_log),
                (resid_mlp, normed_mlp, active, slope),
            )
        )
    resid, final_low = norm_forward(resid, gain_w[3 * levels], part_sum)
    predicted = dot_nt(io_w[1], final_low)
    residual_error = predicted - noise
    snr_ratio = alpha_bar / (1.0 - alpha_bar)
    loss_weight = jnp.minimum(snr_ratio, snr_limit) / snr_ratio
    valid = (item < item_counts[0]).astype(jnp.float32)
    item_scale = valid * loss_weight / (channels * frames)
    loss_part = item_scale * jnp.sum(residual_error * residual_error)
    pred_grad = as_low((2.0 * item_scale / item_total) * residual_error)
    out_proj_grad = dot_nn(pred_grad, final_low)
    final_grad = dot_tn(pred_grad, io_w[1])

    gain_grads = [None] * gain_count
    resid_grad, branch_grad, gain_grads[3 * levels] = norm_backward(
        resid, gain_w[3 * levels], final_grad
    )
    text_grads = [[None] * levels for _ in range(items)]
    for level in reversed(range(levels)):
        kept_self, kept_cross, kept_mlp = kept_all[level]
        resid_mlp, normed_mlp, active, slope = kept_mlp
        flow.add(
            (GRAD + DOWN, level),
            Scatter(layout, [as_low(dot_tn(branch_grad, a)) for a in active], False),
        )
        hidden_grad = [
            as_low(dot_nn(branch_grad, w) * s.astype(jnp.float32))
            for w, s in zip(weight(DOWN, level), slope)
        ]
        hidden_grad = flow.at((AT_HIDDEN_GRAD, level), hidden_grad)
        flow.add(
            (GRAD + UP, level),
            Scatter(layout, [as_low(dot_tn(normed_mlp, z)) for z in hidden_grad], True),
        )
        total = add_terms([dot_nt(z, w) for z, w in zip(hidden_grad, weight(UP, level))])
        (upstream,) = flow.at((AT_MLP_GRAD, level), [as_low(total)])
        resid_grad, branch_grad, gain_grads[3 * level + 2] = norm_backward(
            resid_mlp, gain_w[3 * level + 2], upstream, resid_grad
        )

        resid_cross, normed_cross, cross_query, cross_out, cross_log = kept_cross
        key_at = 2 * level * part
        out_grads = [as_low(dot_nn(branch_grad, w[2])) for w in weight(MID, level)]
        out_grads = flow.at((AT_CROSS_GRAD, level), out_grads)
        cross_w_grad, query_w_grad, query_grads = ([None] * items for _ in range(3))
        for index in reversed(range(items)):
            text = text_kv[index]
            query_grads[index], text_grads[index][level] = attend_backward(
                length,
                cross_query[index],
                0,
                text,
                key_at,
                text,
                key_at + part,
                cross_out[index],
                out_grads[index],
                cross_log[index],
                part,
                True,
            )
            cross_w_grad[index] = dot_tn(branch_grad, cross_out[index])
            query_w_grad[index] = dot_tn(normed_cross, query_grads[index])
        total = add_terms([dot_nt(q, w[1]) for q, w in zip(query_grads, weight(MID, level))])
        (upstream,) = flow.at((AT_CROSSED_GRAD, level), [as_low(total)])
        resid_grad, branch_grad, gain_grads[3 * level + 1] = norm_backward(
            resid_cross, gain_w[3 * level + 1], upstream, resid_grad
        )
        if level == 0:
            flow.add(
                (GRAD + TEXT, 0),
                Scatter(
                    layout,
                    [as_low(dot_tn(text_feat, jnp.concatenate(g, 1))) for g in text_grads],
                    True,
                ),
            )

        resid_self, normed_self, qkv, attended, self_log = kept_self
        self_w_grad = [dot_tn(branch_grad, o) for o in attended]
        flow.add(
            (GRAD + MID, level),
            Scatter(
                layout,
                [
                    as_low(jnp.concatenate(three, 1))
                    for three in zip(self_w_grad, query_w_grad, cross_w_grad)
                ],
                False,
            ),
        )
        out_grads = [as_low(dot_nn(branch_grad, w[0])) for w in weight(MID, level)]
        out_grads = flow.at((AT_SELF_GRAD, level), out_grads)
        qkv_grads = [None] * items
        for index in reversed(range(items)):
            if index == 0:
                out_grads[:1] = flow.at((AT_SELF_GRAD_NEXT, level), out_grads[:1])
            whole = qkv[index]
            (qkv_grads[index],) = attend_backward(
                length,
                whole,
                0,
                whole,
                part,
                whole,
                2 * part,
                attended[index],
                out_grads[index],
                self_log[index],
                part,
                False,
            )
        flow.add(
            (GRAD + QKV, level),
            Scatter(
                layout, [as_low(dot_tn(normed_self, z)) for z in qkv_grads], level > 0
            ),
        )
        total = add_terms([dot_nt(z, w) for z, w in zip(qkv_grads, weight(QKV, level))])
        (upstream,) = flow.at((AT_ATTENDED_GRAD, level), [as_low(total)])
        resid_grad, branch_grad, gain_grads[3 * level] = norm_backward(
            resid_self, gain_w[3 * level], upstream, resid_grad
        )

    down_g, up_g, mid_g, qkv_g = (
        [flow.chunks[name, level].finish() for level in range(levels)]
        for name in (GRAD + DOWN, GRAD + UP, GRAD + MID, GRAD + QKV)
    )
    text_g = flow.chunks[GRAD + TEXT, 0].finish()
    in_proj_grad = dot_nn(noisy, branch_grad)
    small_grad = jnp.concatenate([in_proj_grad, out_proj_grad, jnp.stack(gain_grads)], 0)
    small_grad = small_grad.reshape(-1, layout.dp_size, block).swapaxes(0, 1)
    small_grad = Scatter(layout, [small_grad, small_grad], False).finish()[0]

    io_grad = small_grad[: 2 * channels].reshape(2, channels, block)
    gain_grad = small_grad[2 * channels :]
    col_grad = jnp.stack(
        [
            jnp.concatenate(
                [
                    qkv_g[level].reshape(block, 3, part),
                    mid_g[level][:, None, part : 2 * part],
                    up_g[level].reshape(block, -1, part),
                ],
                1,
            )
            for level in range(levels)
        ]
    )
    kv_grad = jnp.swapaxes(text_g.reshape(text_block, levels, 2, part), 0, 1)
    row_grad = jnp.stack(
        [
            jnp.concatenate(
                [
                    mid_g[level][None, :, :part],
                    mid_g[level][None, :, 2 * part :],
                    jnp.swapaxes(down_g[level].reshape(block, -1, part), 0, 1),
                ],
                0,
            )
            for level in range(levels)
        ]
    )

    first_owner = (item * layout.ranks + layout.rank == 0).astype(jnp.float32)
    square = add_terms(
        [
            jnp.sum(grad * grad)
            for group in (qkv_g, mid_g, up_g, down_g, [text_g])
            for grad in group
        ]
    )
    square = square + first_owner * jnp.sum(small_grad * small_grad)
    loss_part = loss_part * (layout.rank == 0).astype(jnp.float32)
    totals = all_totals(layout, jnp.stack([square, loss_part]))
    grad_norm = jnp.sqrt(totals[0])
    factor = jnp.minimum(1.0, clip_limit / (grad_norm + 1e-06))
    results = [totals[1], item_total, grad_norm]
    io_updated = adam_update(
        io_weight, io_first, io_second, io_average, io_grad, factor, matrix_rate
    )
    results.extend(
        [io_updated[0], io_updated[1], io_updated[2][0], io_updated[2][1], io_updated[3]]
    )
    results.extend(
        adam_update(
            norm_gains, gains_first, gains_second, gains_average, gain_grad, factor, gain_rate
        )
    )
    results.extend(
        adam_update(col_weight, col_first, col_second, col_average, col_grad, factor, matrix_rate)
    )
    results.extend(
        adam_update(
            text_weight, text_first, text_second, text_average, kv_grad, factor, matrix_rate
        )
    )
    results.extend(
        adam_update(row_weight, row_first, row_second, row_average, row_grad, factor, row_rate)
    )
    return tuple(results)


def solution(mesh):
    def step(*arguments):
        dp_size = mesh.shape[DP]
        items = arguments[0].shape[0] // dp_size
        devices = mesh.devices.reshape(dp_size, items, -1)
        return jax.shard_map(
            local,
            mesh=Mesh(devices, (DP, ITEM, RANK)),
            in_specs=(
                P(DP, None, MODEL),
                P(DP, None, MODEL),
                P(DP),
                P(DP, None),
                P(DP),
                P(DP),
                P(MODEL, None),
                P(None, None, DP),
                P(None, None, DP),
                P(None, None, DP),
                P(None, None, DP),
                P(None, DP),
                P(None, DP),
                P(None, DP),
                P(None, DP),
                P(None, DP, None, MODEL),
                P(None, DP, None, MODEL),
                P(None, DP, None, MODEL),
                P(None, DP, None, MODEL),
                P(None, DP, None, MODEL),
                P(None, DP, None, MODEL),
                P(None, DP, None, MODEL),
                P(None, DP, None, MODEL),
                P(None, None, DP, MODEL),
                P(None, None, DP, MODEL),
                P(None, None, DP, MODEL),
                P(None, None, DP, MODEL),
            ),
            out_specs=(
                P(),
                P(),
                P(),
                P(None, None, DP),
                P(None, None, DP),
                P(None, DP),
                P(None, DP),
                P(None, None, DP),
                P(None, DP),
                P(None, DP),
                P(None, DP),
                P(None, DP),
                P(None, DP, None, MODEL),
                P(None, DP, None, MODEL),
                P(None, DP, None, MODEL),
                P(None, DP, None, MODEL),
                P(None, DP, None, MODEL),
                P(None, DP, None, MODEL),
                P(None, DP, None, MODEL),
                P(None, DP, None, MODEL),
                P(None, None, DP, MODEL),
                P(None, None, DP, MODEL),
                P(None, None, DP, MODEL),
                P(None, None, DP, MODEL),
            ),
            check_vma=False,
        )(*arguments)

    return step
```
